768 devices in a mesh: east: 96 (over z_lo, y, x), north: 8 (over z_hi, core).
Axes of the slice: x: 4, y: 8, z: 12 (z_hi: 4, z_lo: 3; z = z_hi * 3 + z_lo), core: 2. Of those that a mesh axis runs over, the one named last changes fastest.
Arguments:
- field_prev: float32 [3, 768, 256, 128], P(None, 'east', 'north'), may hold values from -6 to 6
- field_now: float32 [3, 768, 256, 128], P(None, 'east', 'north'), may hold values from -6 to 6
- speed_sq: float32 [768, 256, 128], P('east', 'north'), may hold values from 0.04 to 0.2
- mechanism: float32 [6, 12288], P(None, ('east', 'north')), may hold values from -6 to 6
- sub_cells: int32 [12288], P(('east', 'north')), may hold values from 0 to 32767
- sub_patch: int32 [12288], P(('east', 'north')), may hold values from 0 to 6143
Outputs:
- field_next: float32 [3, 768, 256, 128], P(None, 'east', 'north')
- field_last: float32 [3, 768, 256, 128], P(None, 'east', 'north')
- patch_grad: float32 [6144], P(('east', 'north'))
The draws below stay inside these ranges and needn't reach their ends.
All inputs are finite; a program needn't handle non-finite values.
Results may differ from the reference program's by a relative error of at most 0.00019.
Values sent between devices are 32-bit elements; how exact they have to be, the bound alone decides.
No kernel may reach another device: no remote copies, remote signals or barrier semaphores. Data moves between devices by JAX's collectives and lax.ppermute only.
A program may use at most 128 MiB of HBM per device.

```python
import math
import jax
import jax.numpy as jnp

CE = 8
CN = 32
CZ = 128
SUB_DEV = 16
NE = 768
NN = 256
NZ = 128
SUB = 12288
PATCH = 6144
N_NORTH = 8


def set_ends(array, rng, smallest, largest):
    shape = array.shape
    index_at = [jax.random.randint(jax.random.fold_in(rng, axis), (), 0, shape[axis]) for axis in range(len(shape))]
    array = array.at[tuple(index_at)].set(smallest)
    longest = shape.index(max(shape))
    index_at[longest] = (index_at[longest] + 1) % shape[longest]
    return array.at[tuple(index_at)].set(largest)


def shard_levels(own_key, extent, shards, least, largest):
    def one(dim, shards_of):
        steps = jax.random.uniform(jax.random.fold_in(jax.random.fold_in(own_key, 6), dim), (shards_of,), jnp.float32, least / len(shards), largest / len(shards))
        return jnp.repeat(jnp.exp(steps), extent[dim] // shards_of).reshape((-1,) + (1,) * (len(extent) - dim - 1))

    gain = one(*shards[0])
    for cut in shards[1:]:
        gain = gain * one(*cut)
    return gain


def normal_values(rng, extent, scale, reach, cuts=(), kind=jnp.bfloat16):
    drawn = jax.random.normal(rng, extent, jnp.float32) * scale
    if len(cuts) > 0:
        drawn = shard_levels(rng, extent, cuts, -0.22, 0.18) * drawn
    return jnp.clip(drawn, min=-reach, max=reach).astype(kind)


def setup_inputs(seed: int = 0) -> dict:
    key_of = jax.random.split(jax.random.key(seed), 7)
    return {
        "field_prev": normal_values(key_of[0], (3, NE, NN, NZ), 1.0, 6.0, ((1, 96), (2, 8)), jnp.float32),
        "field_now": normal_values(key_of[1], (3, NE, NN, NZ), 1.0, 6.0, ((1, 96), (2, 8)), jnp.float32),
        "speed_sq": jnp.clip(jnp.exp(math.log(0.2) - 1.609438 * jax.random.uniform(key_of[2], (NE, NN, NZ), jnp.float32) ** shard_levels(key_of[2], (NE, NN, NZ), ((0, 96), (1, 8)), -0.2, 0.2)), 0.04, 0.2),
        "mechanism": normal_values(key_of[3], (6, SUB), 1.0, 6.0, ((1, 768),), jnp.float32),
        "sub_cells": set_ends(jax.random.randint(key_of[4], (SUB,), 0, CE * CN * CZ), jax.random.fold_in(key_of[4], 1), 0, (CE * CN * CZ) - 1).astype(jnp.int32),
        "sub_patch": set_ends(jax.random.randint(key_of[5], (SUB,), 0, PATCH), jax.random.fold_in(key_of[5], 1), 0, PATCH - 1).astype(jnp.int32),
    }


def second_diff(padded, axis, size):
    def take(offset):
        return jax.lax.slice_in_dim(padded, offset, offset + size, axis=axis)
    return (-take(0) + 16.0 * take(1) - 30.0 * take(2) + 16.0 * take(3) - take(4)) / 12.0


def laplace_valid(field):
    deeper = jnp.pad(field, ((0, 0), (0, 0), (0, 0), (2, 2)))
    east_len = field.shape[1] - 4
    north_len = field.shape[2] - 4
    depth_len = field.shape[3]
    along_east = second_diff(deeper[:, :, 2:2 + north_len, 2:2 + depth_len], 1, east_len)
    along_north = second_diff(deeper[:, 2:2 + east_len, :, 2:2 + depth_len], 2, north_len)
    along_depth = second_diff(deeper[:, 2:2 + east_len, 2:2 + north_len, :], 3, depth_len)
    return along_east + along_north + along_depth


def reference(field_prev, field_now, speed_sq, mechanism, sub_cells, sub_patch):
    widths = ((0, 0), (2, 2), (2, 2), (0, 0))
    field_next = 2.0 * field_now - field_prev + speed_sq[None] * laplace_valid(jnp.pad(field_now, widths))
    field_last = 2.0 * field_next - field_now + speed_sq[None] * laplace_valid(jnp.pad(field_next, widths))
    order = jnp.arange(SUB, dtype=jnp.int32)
    device = order // SUB_DEV
    east_pos = (device // N_NORTH) * CE + sub_cells // (CN * CZ)
    north_pos = (device % N_NORTH) * CN + (sub_cells // CZ) % CN
    depth_pos = sub_cells % CZ
    sample_next = field_next[:, east_pos, north_pos, depth_pos]
    sample_last = field_last[:, east_pos, north_pos, depth_pos]
    grads = jnp.sum(mechanism[0:3] * sample_next + mechanism[3:6] * sample_last, axis=0)
    patch_grad = jax.ops.segment_sum(grads, sub_patch, num_segments=PATCH)
    return field_next, field_last, patch_grad
```

```python
import functools

import jax
import jax.numpy as jnp
from jax import lax
from jax.experimental import pallas as pl
from jax.experimental.pallas import tpu as pltpu
from jax.sharding import PartitionSpec as P

BOTH = ("east", "north")
CE, CN, CZ = 8, 32, 128
SUBS = 16
N_NORTH = 8
PLANE = 32
Z_RUN = 3
COLUMN = Z_RUN * N_NORTH
PATCH_DEV = 8
PER_ROW = CZ // PATCH_DEV
ROWS = PLANE // PER_ROW
VMEM = pl.BlockSpec(memory_space=pltpu.VMEM)
SMEM = pl.BlockSpec(memory_space=pltpu.SMEM)
LIMIT = 32 * 1024 * 1024


def column_groups():
    return [
        [(run * PLANE + at) * N_NORTH + n for run in range(Z_RUN) for n in range(N_NORTH)]
        for at in range(PLANE)
    ]


def plane_groups():
    return [
        [(run * PLANE + at) * N_NORTH + n for at in range(PLANE)]
        for run in range(Z_RUN)
        for n in range(N_NORTH)
    ]


def put_strips(field, east_low, east_high, north_low, north_high):
    for c in range(3):
        east_low[c] = field[c, 0:2]
        east_high[c] = field[c, CE - 2 : CE]
        for e in range(CE):
            at = (c * CE + e) * 2
            north_low[at : at + 2, :] = field[c, e, 0:2, :]
            north_high[at : at + 2, :] = field[c, e, CN - 2 : CN, :]


def strips_kernel(field, east_low, east_high, north_low, north_high):
    put_strips(field, east_low, east_high, north_low, north_high)


def strip_shapes():
    east = jax.ShapeDtypeStruct((3, 2, CN, CZ), jnp.float32)
    north = jax.ShapeDtypeStruct((3 * CE * 2, CZ), jnp.float32)
    return [east, east, north, north]


def step(before, middle, speed_sq, from_west, from_east, from_south, from_north, out, wide):
    lane = lax.broadcasted_iota(jnp.int32, (CN, CZ), 1)

    def component(c, carry):
        for e in range(CE):
            slot = c * CE + e
            at = pl.multiple_of(slot * 2, 2)
            here = middle[c, e]
            wide[slot, 8 : 8 + CN, :] = here
            wide[slot, 6:8, :] = from_south[pl.ds(at, 2), :]
            wide[slot, 8 + CN : 10 + CN, :] = from_north[pl.ds(at, 2), :]

            def layer(k):
                if k < 0:
                    return from_west[c, k + 2]
                if k >= CE:
                    return from_east[c, k - CE]
                return middle[c, k]

            near = layer(e - 1) + layer(e + 1)
            far = layer(e - 2) + layer(e + 2)
            near += wide[slot, 7 : 7 + CN, :] + wide[slot, 9 : 9 + CN, :]
            far += wide[slot, 6 : 6 + CN, :] + wide[slot, 10 : 10 + CN, :]
            near += jnp.where(lane >= 1, pltpu.roll(here, 1, 1), 0.0)
            near += jnp.where(lane < CZ - 1, pltpu.roll(here, CZ - 1, 1), 0.0)
            far += jnp.where(lane >= 2, pltpu.roll(here, 2, 1), 0.0)
            far += jnp.where(lane < CZ - 2, pltpu.roll(here, CZ - 2, 1), 0.0)
            laplace = near * (16.0 / 12.0) - far * (1.0 / 12.0) - here * 7.5
            out[c, e] = 2.0 * here - before[c, e] + speed_sq[e] * laplace
        return carry

    lax.fori_loop(0, 3, component, 0)


def first_kernel(before, middle, speed_sq, w, e, s, n, out, east_low, east_high, north_low, north_high, wide):
    step(before, middle, speed_sq, w, e, s, n, out, wide)
    put_strips(out, east_low, east_high, north_low, north_high)


def second_kernel(before, middle, speed_sq, w, e, s, n, mechanism, cells, patches, out, parts, wide):
    step(before, middle, speed_sq, w, e, s, n, out, wide)
    lane = lax.broadcasted_iota(jnp.int32, (1, CZ), 1)
    parts[...] = jnp.zeros_like(parts)
    for i in range(SUBS):
        cell, patch = cells[i], patches[i]
        layer, row, depth = cell >> 12, (cell >> 7) & (CN - 1), cell & (CZ - 1)
        total = jnp.zeros((1, CZ), jnp.float32)
        for c in range(3):
            total += mechanism[c, i] * middle[c, layer, pl.ds(row, 1), :]
            total += mechanism[3 + c, i] * out[c, layer, pl.ds(row, 1), :]
        total = jnp.where(lane == depth, total, 0.0)
        run, at = patch >> 11, (patch >> 6) & (PLANE - 1)
        place = (at & (PER_ROW - 1)) * PATCH_DEV + (patch & (PATCH_DEV - 1))
        turned = pltpu.roll(total, (place - depth) & (CZ - 1), 1)
        to = run * N_NORTH + ((patch >> 3) & (N_NORTH - 1))
        parts[to, pl.ds(at >> 4, 1), :] += turned


def spread_kernel(parts, out):
    total = jnp.sum(parts[...], axis=0)
    for row in range(ROWS):
        out[row * PER_ROW : (row + 1) * PER_ROW] = jnp.broadcast_to(
            total[row : row + 1][None], (PER_ROW, 1, CZ)
        )


def own_kernel(parts, out):
    total = jnp.sum(parts[...], axis=0)
    at = lax.axis_index("east") & (PER_ROW - 1)
    turned = pltpu.roll(total, (CZ - at * PATCH_DEV) & (CZ - 1), 1)
    out[...] = turned[:, 0:PATCH_DEV]


def path(axis, count, ahead):
    if ahead:
        return functools.partial(lax.ppermute, axis_name=axis, perm=[(i, i + 1) for i in range(count - 1)])
    return functools.partial(lax.ppermute, axis_name=axis, perm=[(i + 1, i) for i in range(count - 1)])


def swap(strips):
    east_low, east_high, north_low, north_high = strips
    n_east, n_north = lax.axis_size("east"), lax.axis_size("north")
    return (
        path("east", n_east, True)(east_high),
        path("east", n_east, False)(east_low),
        path("north", n_north, True)(north_high),
        path("north", n_north, False)(north_low),
    )


def body(field_prev, field_now, speed_sq, mechanism, sub_cells, sub_patch):
    params = pltpu.CompilerParams(vmem_limit_bytes=LIMIT)
    field = jax.ShapeDtypeStruct((3, CE, CN, CZ), jnp.float32)
    wide = pltpu.VMEM((3 * CE, CN + 16, CZ), jnp.float32)
    strips = pl.pallas_call(
        strips_kernel, out_shape=strip_shapes(), in_specs=[VMEM], out_specs=[VMEM] * 4,
        compiler_params=params, name="strips",
    )(field_now)
    halos = swap(strips)
    field_next, *strips = pl.pallas_call(
        first_kernel, out_shape=[field] + strip_shapes(), in_specs=[VMEM] * 7,
        out_specs=[VMEM] * 5, scratch_shapes=[wide], compiler_params=params, name="first",
    )(field_prev, field_now, speed_sq, *halos)
    halos = swap(strips)
    parts = jax.ShapeDtypeStruct((COLUMN, ROWS, CZ), jnp.float32)
    field_last, parts = pl.pallas_call(
        second_kernel, out_shape=[field, parts], in_specs=[VMEM] * 7 + [SMEM] * 3,
        out_specs=[VMEM] * 2, scratch_shapes=[wide], compiler_params=params, name="second",
    )(field_now, field_next, speed_sq, *halos, mechanism, sub_cells, sub_patch)
    parts = lax.all_to_all(parts, BOTH, 0, 0, tiled=True, axis_index_groups=column_groups())
    parts = pl.pallas_call(
        spread_kernel, out_shape=jax.ShapeDtypeStruct((PLANE, 1, CZ), jnp.float32),
        in_specs=[VMEM], out_specs=VMEM, compiler_params=params, name="spread",
    )(parts)
    parts = lax.all_to_all(parts, BOTH, 0, 0, tiled=True, axis_index_groups=plane_groups())
    own = pl.pallas_call(
        own_kernel, out_shape=jax.ShapeDtypeStruct((1, PATCH_DEV), jnp.float32),
        in_specs=[VMEM], out_specs=VMEM, compiler_params=params, name="own",
    )(parts)
    return field_next, field_last, own.reshape(PATCH_DEV)


def solution(mesh):
    in_specs = (
        P(None, "east", "north", None),
        P(None, "east", "north", None),
        P("east", "north", None),
        P(None, BOTH),
        P(BOTH),
        P(BOTH),
    )
    out_specs = (
        P(None, "east", "north", None),
        P(None, "east", "north", None),
        P(BOTH),
    )
    return jax.shard_map(body, mesh=mesh, in_specs=in_specs, out_specs=out_specs, check_vma=False)
```

```python
import jax
import jax.numpy as jnp
from jax import lax
from jax.experimental import pallas as pl
from jax.experimental.pallas import tpu as pltpu
from jax.sharding import PartitionSpec as P

BOTH = ("east", "north")
CE, CN, CZ = 8, 32, 128
SUBS = 16
N_NORTH = 8
PLANE = 32
Z_RUN = 3
COLUMN = Z_RUN * N_NORTH
PATCH_DEV = 8
PER_ROW = CZ // PATCH_DEV
ROWS = PLANE // PER_ROW
VMEM = pl.BlockSpec(memory_space=pltpu.VMEM)
SMEM = pl.BlockSpec(memory_space=pltpu.SMEM)
HBM = pl.BlockSpec(memory_space=pltpu.HBM)
LIMIT = 32 * 1024 * 1024

E_PREV, E_SPEED, E_LEN = 12, 18, 20
N_PREV, N_SPEED, N_LEN = 144, 192, 208
TOP = 16
LAYERS = CE + 4


def column_groups():
    return [
        [(run * PLANE + at) * N_NORTH + n for run in range(Z_RUN) for n in range(N_NORTH)]
        for at in range(PLANE)
    ]


def plane_groups():
    return [
        [(run * PLANE + at) * N_NORTH + n for at in range(PLANE)]
        for run in range(Z_RUN)
        for n in range(N_NORTH)
    ]


def swap(block, axis, first):
    pairs = [(i, i + 1) for i in range(first, lax.axis_size(axis) - 1, 2)]
    return lax.ppermute(block, axis, pairs + [(j, i) for i, j in pairs])


def east_kernel(before, middle, speed_sq, low_pair, high_pair, sems):
    odd = lax.axis_index("east") & 1
    copies = []
    for message, high in ((low_pair, 1 - odd), (high_pair, odd)):
        four, two = high * (CE - 4), high * (CE - 2)
        for c in range(3):
            copies.append((middle.at[c, pl.ds(four, 4)], message.at[pl.ds(c * 4, 4)]))
            copies.append((before.at[c, pl.ds(two, 2)], message.at[pl.ds(E_PREV + c * 2, 2)]))
        copies.append((speed_sq.at[pl.ds(two, 2)], message.at[pl.ds(E_SPEED, 2)]))
    started = [pltpu.make_async_copy(a, b, sems.at[i]) for i, (a, b) in enumerate(copies)]
    for copy in started:
        copy.start()
    for copy in started:
        copy.wait()


def east_layers(low_pair, high_pair):
    odd = (lax.axis_index("east") & 1) == 1

    def west(k, rows=slice(None)):
        return jnp.where(odd, low_pair[k, rows], high_pair[k, rows])

    def east(k, rows=slice(None)):
        return jnp.where(odd, high_pair[k, rows], low_pair[k, rows])

    return west, east


def north_kernel(before, middle, speed_sq, low_pair, high_pair, near, far):
    odd = (lax.axis_index("north") & 1) == 1
    west, east = east_layers(low_pair, high_pair)

    def put(at, count, low, high):
        near[at : at + count, :] = jnp.where(odd, low, high)
        far[at : at + count, :] = jnp.where(odd, high, low)

    bottom, top = slice(0, 4), slice(CN - 4, CN)
    for c in range(3):
        for k in range(2):
            put((c * LAYERS + k) * 4, 4, west(c * 4 + 2 + k, bottom), west(c * 4 + 2 + k, top))
            put((c * LAYERS + CE + 2 + k) * 4, 4, east(c * 4 + k, bottom), east(c * 4 + k, top))
        for e in range(CE):
            put((c * LAYERS + 2 + e) * 4, 4, middle[c, e, 0:4, :], middle[c, e, CN - 4 : CN, :])
            put(N_PREV + (c * CE + e) * 2, 2, before[c, e, 0:2, :], before[c, e, CN - 2 : CN, :])
    for e in range(CE):
        put(N_SPEED + e * 2, 2, speed_sq[e, 0:2, :], speed_sq[e, CN - 2 : CN, :])


def laplace(here, near, far):
    lane = lax.broadcasted_iota(jnp.int32, here.shape, 1)
    near += jnp.where(lane >= 1, pltpu.roll(here, 1, 1), 0.0)
    near += jnp.where(lane < CZ - 1, pltpu.roll(here, CZ - 1, 1), 0.0)
    far += jnp.where(lane >= 2, pltpu.roll(here, 2, 1), 0.0)
    far += jnp.where(lane < CZ - 2, pltpu.roll(here, CZ - 2, 1), 0.0)
    return near * (16.0 / 12.0) - far * (1.0 / 12.0) - here * 7.5


def steps_kernel(
    before, middle, speed_sq, low_pair, high_pair, near_pair, far_pair, mechanism, cells, patches,
    field_next, field_last, parts, wide, later, edge_before, edge_speed,
):
    west, east = east_layers(low_pair, high_pair)
    odd_north = (lax.axis_index("north") & 1) == 1

    def south(at, count):
        return jnp.where(odd_north, near_pair[pl.ds(at, count), :], far_pair[pl.ds(at, count), :])

    def north(at, count):
        return jnp.where(odd_north, far_pair[pl.ds(at, count), :], near_pair[pl.ds(at, count), :])

    for e in range(CE):
        edge_speed[e, 6:8, :] = south(N_SPEED + e * 2, 2)
        edge_speed[e, 8:10, :] = north(N_SPEED + e * 2, 2)

    def first(c, carry):
        def layer(k):
            if k < 0:
                return west(c * 4 + k + 4)
            if k >= CE:
                return east(c * 4 + k - CE)
            return middle[c, k]

        for e in range(-2, CE + 2):
            k = e + 2
            at = pl.multiple_of((c * LAYERS + k) * 4, 4)
            wide[c, k, TOP : TOP + CN, :] = layer(e)
            wide[c, k, TOP - 4 : TOP, :] = south(at, 4)
            wide[c, k, TOP + CN : TOP + CN + 4, :] = north(at, 4)
        for e in range(-2, CE + 2):
            k = e + 2

            def rows(offset, count=CN):
                return wide[c, k, TOP + offset : TOP + offset + count, :]

            here = rows(0)
            total = laplace(
                here,
                layer(e - 1) + layer(e + 1) + rows(-1) + rows(1),
                layer(e - 2) + layer(e + 2) + rows(-2) + rows(2),
            )
            if 0 <= e < CE:
                old, speed = before[c, e], speed_sq[e]
            elif e < 0:
                old, speed = west(E_PREV + c * 2 + k), west(E_SPEED + k)
            else:
                old, speed = east(E_PREV + c * 2 + e - CE), east(E_SPEED + e - CE)
            new = 2.0 * here - old + speed * total
            later[c, k, TOP : TOP + CN, :] = new
            if 0 <= e < CE:
                field_next[c, e] = new
        for e in range(CE):
            k = e + 2
            at = pl.multiple_of(N_PREV + (c * CE + e) * 2, 2)
            edge_before[k, 6:8, :] = south(at, 2)
            edge_before[k, 8:10, :] = north(at, 2)
            for start, edge, kept in ((TOP - 8, 0, slice(6, 8)), (TOP + CN, 8, slice(0, 2))):

                def tile(layers, offset):
                    return wide[c, k + layers, start + offset : start + offset + 8, :]

                here = tile(0, 0)
                total = laplace(
                    here,
                    tile(-1, 0) + tile(1, 0) + tile(0, -1) + tile(0, 1),
                    tile(-2, 0) + tile(2, 0) + tile(0, -2) + tile(0, 2),
                )
                old, speed = edge_before[k, edge : edge + 8, :], edge_speed[e, edge : edge + 8, :]
                new = 2.0 * here - old + speed * total
                later[c, k, start + kept.start : start + kept.stop, :] = new[kept]
        return carry

    lax.fori_loop(0, 3, first, 0)

    def second(c, carry):
        for e in range(CE):
            k = e + 2

            def rows(layers, offset=0):
                return later[c, k + layers, TOP + offset : TOP + offset + CN, :]

            here = rows(0)
            total = laplace(
                here,
                rows(-1) + rows(1) + rows(0, -1) + rows(0, 1),
                rows(-2) + rows(2) + rows(0, -2) + rows(0, 2),
            )
            field_last[c, e] = 2.0 * here - middle[c, e] + speed_sq[e] * total
        return carry

    lax.fori_loop(0, 3, second, 0)

    lane = lax.broadcasted_iota(jnp.int32, (1, CZ), 1)
    parts[...] = jnp.zeros_like(parts)
    for i in range(SUBS):
        cell, patch = cells[i], patches[i]
        layer, row, depth = cell >> 12, (cell >> 7) & (CN - 1), cell & (CZ - 1)
        total = jnp.zeros((1, CZ), jnp.float32)
        for c in range(3):
            total += mechanism[c, i] * field_next[c, layer, pl.ds(row, 1), :]
            total += mechanism[3 + c, i] * field_last[c, layer, pl.ds(row, 1), :]
        total = jnp.where(lane == depth, total, 0.0)
        run, at = patch >> 11, (patch >> 6) & (PLANE - 1)
        place = (at & (PER_ROW - 1)) * PATCH_DEV + (patch & (PATCH_DEV - 1))
        turned = pltpu.roll(total, (place - depth) & (CZ - 1), 1)
        to = run * N_NORTH + ((patch >> 3) & (N_NORTH - 1))
        parts[to, pl.ds(at >> 4, 1), :] += turned


def spread_kernel(parts, out):
    total = jnp.sum(parts[...], axis=0)
    for row in range(ROWS):
        out[row * PER_ROW : (row + 1) * PER_ROW] = jnp.broadcast_to(
            total[row : row + 1][None], (PER_ROW, 1, CZ)
        )


def own_kernel(parts, out):
    total = jnp.sum(parts[...], axis=0)
    at = lax.axis_index("east") & (PER_ROW - 1)
    turned = pltpu.roll(total, (CZ - at * PATCH_DEV) & (CZ - 1), 1)
    out[...] = turned[:, 0:PATCH_DEV]


def body(field_prev, field_now, speed_sq, mechanism, sub_cells, sub_patch):
    params = pltpu.CompilerParams(vmem_limit_bytes=LIMIT)
    f32 = jnp.float32
    field = jax.ShapeDtypeStruct((3, CE, CN, CZ), f32)
    message = jax.ShapeDtypeStruct((E_LEN, CN, CZ), f32)
    low_pair, high_pair = pl.pallas_call(
        east_kernel, out_shape=[message] * 2, in_specs=[HBM] * 3, out_specs=[VMEM] * 2,
        scratch_shapes=[pltpu.SemaphoreType.DMA((14,))], compiler_params=params, name="east_strips",
    )(field_prev, field_now, speed_sq)
    pairs = swap(low_pair, "east", 0), swap(high_pair, "east", 1)
    message = jax.ShapeDtypeStruct((N_LEN, CZ), f32)
    near, far = pl.pallas_call(
        north_kernel, out_shape=[message] * 2, in_specs=[VMEM] * 5, out_specs=[VMEM] * 2,
        compiler_params=params, name="north_strips",
    )(field_prev, field_now, speed_sq, *pairs)
    far_pair = swap(far, "north", 1)
    near_pair = swap(near, "north", 0)
    wide = pltpu.VMEM((3, LAYERS, CN + 2 * TOP, CZ), f32)
    parts = jax.ShapeDtypeStruct((COLUMN, ROWS, CZ), f32)
    field_next, field_last, parts = pl.pallas_call(
        steps_kernel, out_shape=[field, field, parts], in_specs=[VMEM] * 7 + [SMEM] * 3,
        out_specs=[VMEM] * 3,
        scratch_shapes=[wide, wide, pltpu.VMEM((LAYERS, 16, CZ), f32), pltpu.VMEM((CE, 16, CZ), f32)],
        compiler_params=params, name="steps",
    )(field_prev, field_now, speed_sq, *pairs, near_pair, far_pair, mechanism, sub_cells, sub_patch)
    parts = lax.all_to_all(parts, BOTH, 0, 0, tiled=True, axis_index_groups=column_groups())
    parts = pl.pallas_call(
        spread_kernel, out_shape=jax.ShapeDtypeStruct((PLANE, 1, CZ), f32),
        in_specs=[VMEM], out_specs=VMEM, compiler_params=params, name="spread",
    )(parts)
    parts = lax.all_to_all(parts, BOTH, 0, 0, tiled=True, axis_index_groups=plane_groups())
    own = pl.pallas_call(
        own_kernel, out_shape=jax.ShapeDtypeStruct((1, PATCH_DEV), f32),
        in_specs=[VMEM], out_specs=VMEM, compiler_params=params, name="own",
    )(parts)
    return field_next, field_last, own.reshape(PATCH_DEV)


def solution(mesh):
    in_specs = (
        P(None, "east", "north", None),
        P(None, "east", "north", None),
        P("east", "north", None),
        P(None, BOTH),
        P(BOTH),
        P(BOTH),
    )
    out_specs = (
        P(None, "east", "north", None),
        P(None, "east", "north", None),
        P(BOTH),
    )
    return jax.shard_map(body, mesh=mesh, in_specs=in_specs, out_specs=out_specs, check_vma=False)
```

```python
import jax
import jax.numpy as jnp
from jax import lax
from jax.experimental import pallas as pl
from jax.experimental.pallas import tpu as pltpu
from jax.sharding import PartitionSpec as P

BOTH = ("east", "north")
CE, CN, CZ = 8, 32, 128
SUBS = 16
N_NORTH = 8
PLANE = 32
Z_RUN = 3
COLUMN = Z_RUN * N_NORTH
PATCH_DEV = 8
PER_ROW = CZ // PATCH_DEV
ROWS = PLANE // PER_ROW
VMEM = pl.BlockSpec(memory_space=pltpu.VMEM)
SMEM = pl.BlockSpec(memory_space=pltpu.SMEM)
HBM = pl.BlockSpec(memory_space=pltpu.HBM)
LIMIT = 32 * 1024 * 1024

E_PREV, E_SPEED, E_LEN = 12, 18, 20
N_PREV, N_SPEED, N_LEN = 96, 144, 160
C_LEN = 24
TOP = 16
LAYERS = CE + 4


def column_groups():
    return [
        [(run * PLANE + at) * N_NORTH + n for run in range(Z_RUN) for n in range(N_NORTH)]
        for at in range(PLANE)
    ]


def plane_groups():
    return [
        [(run * PLANE + at) * N_NORTH + n for at in range(PLANE)]
        for run in range(Z_RUN)
        for n in range(N_NORTH)
    ]


def swap(block, axis, first):
    pairs = [(i, i + 1) for i in range(first, lax.axis_size(axis) - 1, 2)]
    return lax.ppermute(block, axis, pairs + [(j, i) for i, j in pairs])


def load_kernel(
    before, middle, speed_sq, before_here, middle_here, speed_here, low_pair, high_pair, near, far, sems
):
    odd = lax.axis_index("east") & 1
    copies = [(middle, middle_here), (before, before_here), (speed_sq, speed_here)]
    for message, high in ((low_pair, 1 - odd), (high_pair, odd)):
        four, two = high * (CE - 4), high * (CE - 2)
        for c in range(3):
            copies.append((middle.at[c, pl.ds(four, 4)], message.at[pl.ds(c * 4, 4)]))
            copies.append((before.at[c, pl.ds(two, 2)], message.at[pl.ds(E_PREV + c * 2, 2)]))
        copies.append((speed_sq.at[pl.ds(two, 2)], message.at[pl.ds(E_SPEED, 2)]))
    started = [pltpu.make_async_copy(a, b, sems.at[i]) for i, (a, b) in enumerate(copies)]
    for copy in started:
        copy.start()
    for copy in started[:3]:
        copy.wait()
    odd_north = (lax.axis_index("north") & 1) == 1

    def put(at, count, low, high):
        near[at : at + count, :] = jnp.where(odd_north, low, high)
        far[at : at + count, :] = jnp.where(odd_north, high, low)

    for e in range(CE):
        for c in range(3):
            slot = c * CE + e
            put(slot * 4, 4, middle_here[c, e, 0:4, :], middle_here[c, e, CN - 4 : CN, :])
            put(N_PREV + slot * 2, 2, before_here[c, e, 0:2, :], before_here[c, e, CN - 2 : CN, :])
        put(N_SPEED + e * 2, 2, speed_here[e, 0:2, :], speed_here[e, CN - 2 : CN, :])
    for copy in started[3:]:
        copy.wait()


def east_layers(low_pair, high_pair):
    odd = (lax.axis_index("east") & 1) == 1

    def west(k):
        return jnp.where(odd, low_pair[k], high_pair[k])

    def east(k):
        return jnp.where(odd, high_pair[k], low_pair[k])

    return west, east


def north_rows(near_pair, far_pair):
    odd = (lax.axis_index("north") & 1) == 1

    def south(at, count):
        return jnp.where(odd, near_pair[pl.ds(at, count), :], far_pair[pl.ds(at, count), :])

    def north(at, count):
        return jnp.where(odd, far_pair[pl.ds(at, count), :], near_pair[pl.ds(at, count), :])

    return south, north


def corner_kernel(near_pair, far_pair, low_pair, high_pair):
    odd = (lax.axis_index("east") & 1) == 1
    south, north = north_rows(near_pair, far_pair)
    for c in range(3):
        for k in range(2):
            at = (c * 2 + k) * 4
            low, high = (c * CE + k) * 4, (c * CE + CE - 2 + k) * 4
            for rows, lows, highs in (
                (slice(at, at + 2), south(low + 2, 2), south(high + 2, 2)),
                (slice(at + 2, at + 4), north(low, 2), north(high, 2)),
            ):
                low_pair[rows, :] = jnp.where(odd, lows, highs)
                high_pair[rows, :] = jnp.where(odd, highs, lows)


def laplace(here, near, far):
    lane = lax.broadcasted_iota(jnp.int32, here.shape, 1)
    near += jnp.where(lane >= 1, pltpu.roll(here, 1, 1), 0.0)
    near += jnp.where(lane < CZ - 1, pltpu.roll(here, CZ - 1, 1), 0.0)
    far += jnp.where(lane >= 2, pltpu.roll(here, 2, 1), 0.0)
    far += jnp.where(lane < CZ - 2, pltpu.roll(here, CZ - 2, 1), 0.0)
    return near * (16.0 / 12.0) - far * (1.0 / 12.0) - here * 7.5


def steps_kernel(
    before, middle, speed_sq, low_pair, high_pair, near_pair, far_pair, low_corner, high_corner,
    mechanism, cells, patches, field_next, field_last, parts, wide, later, edge_before, edge_speed,
):
    west, east = east_layers(low_pair, high_pair)
    south, north = north_rows(near_pair, far_pair)
    odd = (lax.axis_index("east") & 1) == 1

    for e in range(CE):
        edge_speed[e, 6:8, :] = south(N_SPEED + e * 2, 2)
        edge_speed[e, 8:10, :] = north(N_SPEED + e * 2, 2)

    def first(c, carry):
        def layer(k):
            if k < 0:
                return west(c * 4 + k + 4)
            if k >= CE:
                return east(c * 4 + k - CE)
            return middle[c, k]

        for e in range(-2, CE + 2):
            k = e + 2
            wide[c, k, TOP : TOP + CN, :] = layer(e)
            if 0 <= e < CE:
                at = pl.multiple_of((c * CE + e) * 4, 4)
                wide[c, k, TOP - 4 : TOP, :] = south(at, 4)
                wide[c, k, TOP + CN : TOP + CN + 4, :] = north(at, 4)
            else:
                at = pl.multiple_of((c * 2 + e % CE % 6) * 4, 4)
                low, high = low_corner[pl.ds(at, 4), :], high_corner[pl.ds(at, 4), :]
                corner = jnp.where(odd, low, high) if e < 0 else jnp.where(odd, high, low)
                wide[c, k, TOP - 2 : TOP, :] = corner[0:2]
                wide[c, k, TOP + CN : TOP + CN + 2, :] = corner[2:4]
        for e in range(-2, CE + 2):
            k = e + 2

            def rows(offset, count=CN):
                return wide[c, k, TOP + offset : TOP + offset + count, :]

            here = rows(0)
            total = laplace(
                here,
                layer(e - 1) + layer(e + 1) + rows(-1) + rows(1),
                layer(e - 2) + layer(e + 2) + rows(-2) + rows(2),
            )
            if 0 <= e < CE:
                old, speed = before[c, e], speed_sq[e]
            elif e < 0:
                old, speed = west(E_PREV + c * 2 + k), west(E_SPEED + k)
            else:
                old, speed = east(E_PREV + c * 2 + e - CE), east(E_SPEED + e - CE)
            new = 2.0 * here - old + speed * total
            later[c, k, TOP : TOP + CN, :] = new
            if 0 <= e < CE:
                field_next[c, e] = new
        for e in range(CE):
            k = e + 2
            at = pl.multiple_of(N_PREV + (c * CE + e) * 2, 2)
            edge_before[k, 6:8, :] = south(at, 2)
            edge_before[k, 8:10, :] = north(at, 2)
            for start, edge, kept in ((TOP - 8, 0, slice(6, 8)), (TOP + CN, 8, slice(0, 2))):

                def tile(layers, offset):
                    return wide[c, k + layers, start + offset : start + offset + 8, :]

                here = tile(0, 0)
                total = laplace(
                    here,
                    tile(-1, 0) + tile(1, 0) + tile(0, -1) + tile(0, 1),
                    tile(-2, 0) + tile(2, 0) + tile(0, -2) + tile(0, 2),
                )
                old, speed = edge_before[k, edge : edge + 8, :], edge_speed[e, edge : edge + 8, :]
                new = 2.0 * here - old + speed * total
                later[c, k, start + kept.start : start + kept.stop, :] = new[kept]
        return carry

    lax.fori_loop(0, 3, first, 0)

    def second(c, carry):
        for e in range(CE):
            k = e + 2

            def rows(layers, offset=0):
                return later[c, k + layers, TOP + offset : TOP + offset + CN, :]

            here = rows(0)
            total = laplace(
                here,
                rows(-1) + rows(1) + rows(0, -1) + rows(0, 1),
                rows(-2) + rows(2) + rows(0, -2) + rows(0, 2),
            )
            field_last[c, e] = 2.0 * here - middle[c, e] + speed_sq[e] * total
        return carry

    lax.fori_loop(0, 3, second, 0)

    lane = lax.broadcasted_iota(jnp.int32, (1, CZ), 1)
    parts[...] = jnp.zeros_like(parts)
    for i in range(SUBS):
        cell, patch = cells[i], patches[i]
        layer, row, depth = cell >> 12, (cell >> 7) & (CN - 1), cell & (CZ - 1)
        total = jnp.zeros((1, CZ), jnp.float32)
        for c in range(3):
            total += mechanism[c, i] * field_next[c, layer, pl.ds(row, 1), :]
            total += mechanism[3 + c, i] * field_last[c, layer, pl.ds(row, 1), :]
        total = jnp.where(lane == depth, total, 0.0)
        run, at = patch >> 11, (patch >> 6) & (PLANE - 1)
        place = (at & (PER_ROW - 1)) * PATCH_DEV + (patch & (PATCH_DEV - 1))
        turned = pltpu.roll(total, (place - depth) & (CZ - 1), 1)
        to = run * N_NORTH + ((patch >> 3) & (N_NORTH - 1))
        parts[to, pl.ds(at >> 4, 1), :] += turned


def spread_kernel(parts, out):
    total = jnp.sum(parts[...], axis=0)
    for row in range(ROWS):
        out[row * PER_ROW : (row + 1) * PER_ROW] = jnp.broadcast_to(
            total[row : row + 1][None], (PER_ROW, 1, CZ)
        )


def own_kernel(parts, out):
    total = jnp.sum(parts[...], axis=0)
    at = lax.axis_index("east") & (PER_ROW - 1)
    turned = pltpu.roll(total, (CZ - at * PATCH_DEV) & (CZ - 1), 1)
    out[...] = turned[:, 0:PATCH_DEV]


def body(field_prev, field_now, speed_sq, mechanism, sub_cells, sub_patch):
    params = pltpu.CompilerParams(vmem_limit_bytes=LIMIT)
    f32 = jnp.float32
    field = jax.ShapeDtypeStruct((3, CE, CN, CZ), f32)
    held = (
        pltpu.VMEM((3, CE, CN, CZ), f32), pltpu.VMEM((3, CE, CN, CZ), f32), pltpu.VMEM((CE, CN, CZ), f32)
    )
    east_message, north_message = pltpu.VMEM((E_LEN, CN, CZ), f32), pltpu.VMEM((N_LEN, CZ), f32)
    inputs = [pltpu.with_memory_space_constraint(x, pltpu.HBM) for x in (field_prev, field_now, speed_sq)]
    field_prev, field_now, speed_sq, low_pair, high_pair, near, far = pl.pallas_call(
        load_kernel, out_shape=[*held] + [east_message] * 2 + [north_message] * 2,
        in_specs=[HBM] * 3, out_specs=[VMEM] * 7,
        scratch_shapes=[pltpu.SemaphoreType.DMA((17,))], compiler_params=params, name="load",
    )(*inputs)
    near_pair, far_pair = swap(near, "north", 0), swap(far, "north", 1)
    pairs = swap(low_pair, "east", 0), swap(high_pair, "east", 1)
    low_corner, high_corner = pl.pallas_call(
        corner_kernel, out_shape=[pltpu.VMEM((C_LEN, CZ), f32)] * 2, in_specs=[VMEM] * 2,
        out_specs=[VMEM] * 2, compiler_params=params, name="corners",
    )(near_pair, far_pair)
    corners = swap(low_corner, "east", 0), swap(high_corner, "east", 1)
    wide = pltpu.VMEM((3, LAYERS, CN + 2 * TOP, CZ), f32)
    parts = jax.ShapeDtypeStruct((COLUMN, ROWS, CZ), f32)
    field_next, field_last, parts = pl.pallas_call(
        steps_kernel, out_shape=[field, field, parts], in_specs=[VMEM] * 9 + [SMEM] * 3,
        out_specs=[VMEM] * 3,
        scratch_shapes=[wide, wide, pltpu.VMEM((LAYERS, 16, CZ), f32), pltpu.VMEM((CE, 16, CZ), f32)],
        compiler_params=params, name="steps",
    )(field_prev, field_now, speed_sq, *pairs, near_pair, far_pair, *corners, mechanism, sub_cells, sub_patch)
    parts = lax.all_to_all(parts, BOTH, 0, 0, tiled=True, axis_index_groups=column_groups())
    parts = pl.pallas_call(
        spread_kernel, out_shape=jax.ShapeDtypeStruct((PLANE, 1, CZ), f32),
        in_specs=[VMEM], out_specs=VMEM, compiler_params=params, name="spread",
    )(parts)
    parts = lax.all_to_all(parts, BOTH, 0, 0, tiled=True, axis_index_groups=plane_groups())
    own = pl.pallas_call(
        own_kernel, out_shape=jax.ShapeDtypeStruct((1, PATCH_DEV), f32),
        in_specs=[VMEM], out_specs=VMEM, compiler_params=params, name="own",
    )(parts)
    return field_next, field_last, own.reshape(PATCH_DEV)


def solution(mesh):
    in_specs = (
        P(None, "east", "north", None),
        P(None, "east", "north", None),
        P("east", "north", None),
        P(None, BOTH),
        P(BOTH),
        P(BOTH),
    )
    out_specs = (
        P(None, "east", "north", None),
        P(None, "east", "north", None),
        P(BOTH),
    )
    return jax.shard_map(body, mesh=mesh, in_specs=in_specs, out_specs=out_specs, check_vma=False)
```

```python
import jax
import jax.numpy as jnp
from jax import lax
from jax.experimental import pallas as pl
from jax.experimental.pallas import tpu as pltpu
from jax.sharding import PartitionSpec as P

BOTH = ("east", "north")
CE, CN, CZ = 8, 32, 128
SUBS = 16
N_NORTH = 8
PLANE = 32
Z_RUN = 3
COLUMN = Z_RUN * N_NORTH
PATCH_DEV = 8
PER_ROW = CZ // PATCH_DEV
ROWS = PLANE // PER_ROW
VMEM = pl.BlockSpec(memory_space=pltpu.VMEM)
SMEM = pl.BlockSpec(memory_space=pltpu.SMEM)
HBM = pl.BlockSpec(memory_space=pltpu.HBM)
LIMIT = 32 * 1024 * 1024

E_PREV, E_SPEED, E_LEN = 12, 18, 20
N_PREV, N_SPEED, N_LEN = 96, 144, 160
C_LEN = 24
TOP = 16
LAYERS = CE + 4


def column_groups():
    return [
        [(run * PLANE + at) * N_NORTH + n for run in range(Z_RUN) for n in range(N_NORTH)]
        for at in range(PLANE)
    ]


def plane_groups():
    return [
        [(run * PLANE + at) * N_NORTH + n for at in range(PLANE)]
        for run in range(Z_RUN)
        for n in range(N_NORTH)
    ]


def swap(block, axis, first):
    pairs = [(i, i + 1) for i in range(first, lax.axis_size(axis) - 1, 2)]
    return lax.ppermute(block, axis, pairs + [(j, i) for i, j in pairs])


def load_kernel(
    before, middle, speed_sq, before_here, middle_here, speed_here, far, near, low_pair, high_pair, sems
):
    odd = lax.axis_index("east") & 1
    copies = [(middle, middle_here), (before, before_here), (speed_sq, speed_here)]
    for message, high in ((low_pair, 1 - odd), (high_pair, odd)):
        four, two = high * (CE - 4), high * (CE - 2)
        for c in range(3):
            copies.append((middle.at[c, pl.ds(four, 4)], message.at[pl.ds(c * 4, 4)]))
            copies.append((before.at[c, pl.ds(two, 2)], message.at[pl.ds(E_PREV + c * 2, 2)]))
        copies.append((speed_sq.at[pl.ds(two, 2)], message.at[pl.ds(E_SPEED, 2)]))
    started = [pltpu.make_async_copy(a, b, sems.at[i]) for i, (a, b) in enumerate(copies)]
    for copy in started:
        copy.start()
    for copy in started[:3]:
        copy.wait()
    odd_north = (lax.axis_index("north") & 1) == 1

    def put(at, count, low, high):
        near[at : at + count, :] = jnp.where(odd_north, low, high)
        far[at : at + count, :] = jnp.where(odd_north, high, low)

    for e in range(CE):
        for c in range(3):
            slot = c * CE + e
            put(slot * 4, 4, middle_here[c, e, 0:4, :], middle_here[c, e, CN - 4 : CN, :])
            put(N_PREV + slot * 2, 2, before_here[c, e, 0:2, :], before_here[c, e, CN - 2 : CN, :])
        put(N_SPEED + e * 2, 2, speed_here[e, 0:2, :], speed_here[e, CN - 2 : CN, :])
    for copy in started[3:]:
        copy.wait()


def east_layers(low_pair, high_pair):
    odd = (lax.axis_index("east") & 1) == 1

    def west(k):
        return jnp.where(odd, low_pair[k], high_pair[k])

    def east(k):
        return jnp.where(odd, high_pair[k], low_pair[k])

    return west, east


def north_rows(near_pair, far_pair):
    odd = (lax.axis_index("north") & 1) == 1

    def south(at, count):
        return jnp.where(odd, near_pair[pl.ds(at, count), :], far_pair[pl.ds(at, count), :])

    def north(at, count):
        return jnp.where(odd, far_pair[pl.ds(at, count), :], near_pair[pl.ds(at, count), :])

    return south, north


def corner_kernel(far_pair, near_pair, low_pair, high_pair):
    odd = (lax.axis_index("east") & 1) == 1
    south, north = north_rows(near_pair, far_pair)
    for c in range(3):
        for k in range(2):
            at = (c * 2 + k) * 4
            low, high = (c * CE + k) * 4, (c * CE + CE - 2 + k) * 4
            for rows, lows, highs in (
                (slice(at, at + 2), south(low + 2, 2), south(high + 2, 2)),
                (slice(at + 2, at + 4), north(low, 2), north(high, 2)),
            ):
                low_pair[rows, :] = jnp.where(odd, lows, highs)
                high_pair[rows, :] = jnp.where(odd, highs, lows)


def laplace(here, near, far):
    lane = lax.broadcasted_iota(jnp.int32, here.shape, 1)
    near += jnp.where(lane >= 1, pltpu.roll(here, 1, 1), 0.0)
    near += jnp.where(lane < CZ - 1, pltpu.roll(here, CZ - 1, 1), 0.0)
    far += jnp.where(lane >= 2, pltpu.roll(here, 2, 1), 0.0)
    far += jnp.where(lane < CZ - 2, pltpu.roll(here, CZ - 2, 1), 0.0)
    return near * (16.0 / 12.0) - far * (1.0 / 12.0) - here * 7.5


def steps_kernel(
    before, middle, speed_sq, far_pair, near_pair, low_pair, high_pair, low_corner, high_corner,
    mechanism_far, cells_far, patches_far, next_out, last_out, parts,
    wide, later, field_last, edge_before, edge_speed, mechanism, cells, patches, sub_sems, out_sems,
):
    subs = [
        pltpu.make_async_copy(a, b, sub_sems.at[i])
        for i, (a, b) in enumerate(
            ((mechanism_far, mechanism), (cells_far, cells), (patches_far, patches))
        )
    ]
    for copy in subs:
        copy.start()

    def next_copy(c):
        own = later.at[c, pl.ds(2, CE), pl.ds(TOP, CN)]
        return pltpu.make_async_copy(own, next_out.at[c], out_sems.at[c])

    def last_copy(c):
        return pltpu.make_async_copy(field_last.at[c], last_out.at[c], out_sems.at[3 + c])

    west, east = east_layers(low_pair, high_pair)
    south, north = north_rows(near_pair, far_pair)
    odd = (lax.axis_index("east") & 1) == 1

    for e in range(CE):
        edge_speed[e, 6:8, :] = south(N_SPEED + e * 2, 2)
        edge_speed[e, 8:10, :] = north(N_SPEED + e * 2, 2)

    def first(c, carry):
        def layer(k):
            if k < 0:
                return west(c * 4 + k + 4)
            if k >= CE:
                return east(c * 4 + k - CE)
            return middle[c, k]

        for e in range(-2, CE + 2):
            k = e + 2
            wide[c, k, TOP : TOP + CN, :] = layer(e)
            if 0 <= e < CE:
                at = pl.multiple_of((c * CE + e) * 4, 4)
                wide[c, k, TOP - 4 : TOP, :] = south(at, 4)
                wide[c, k, TOP + CN : TOP + CN + 4, :] = north(at, 4)
            else:
                at = pl.multiple_of((c * 2 + e % CE % 6) * 4, 4)
                low, high = low_corner[pl.ds(at, 4), :], high_corner[pl.ds(at, 4), :]
                corner = jnp.where(odd, low, high) if e < 0 else jnp.where(odd, high, low)
                wide[c, k, TOP - 2 : TOP, :] = corner[0:2]
                wide[c, k, TOP + CN : TOP + CN + 2, :] = corner[2:4]
        for e in range(-2, CE + 2):
            k = e + 2

            def rows(offset, count=CN):
                return wide[c, k, TOP + offset : TOP + offset + count, :]

            here = rows(0)
            total = laplace(
                here,
                layer(e - 1) + layer(e + 1) + rows(-1) + rows(1),
                layer(e - 2) + layer(e + 2) + rows(-2) + rows(2),
            )
            if 0 <= e < CE:
                old, speed = before[c, e], speed_sq[e]
            elif e < 0:
                old, speed = west(E_PREV + c * 2 + k), west(E_SPEED + k)
            else:
                old, speed = east(E_PREV + c * 2 + e - CE), east(E_SPEED + e - CE)
            new = 2.0 * here - old + speed * total
            later[c, k, TOP : TOP + CN, :] = new
        next_copy(c).start()
        for e in range(CE):
            k = e + 2
            at = pl.multiple_of(N_PREV + (c * CE + e) * 2, 2)
            edge_before[k, 6:8, :] = south(at, 2)
            edge_before[k, 8:10, :] = north(at, 2)
            for start, edge, kept in ((TOP - 8, 0, slice(6, 8)), (TOP + CN, 8, slice(0, 2))):

                def tile(layers, offset):
                    return wide[c, k + layers, start + offset : start + offset + 8, :]

                here = tile(0, 0)
                total = laplace(
                    here,
                    tile(-1, 0) + tile(1, 0) + tile(0, -1) + tile(0, 1),
                    tile(-2, 0) + tile(2, 0) + tile(0, -2) + tile(0, 2),
                )
                old, speed = edge_before[k, edge : edge + 8, :], edge_speed[e, edge : edge + 8, :]
                new = 2.0 * here - old + speed * total
                later[c, k, start + kept.start : start + kept.stop, :] = new[kept]
        return carry

    lax.fori_loop(0, 3, first, 0)

    def second(c, carry):
        for e in range(CE):
            k = e + 2

            def rows(layers, offset=0):
                return later[c, k + layers, TOP + offset : TOP + offset + CN, :]

            here = rows(0)
            total = laplace(
                here,
                rows(-1) + rows(1) + rows(0, -1) + rows(0, 1),
                rows(-2) + rows(2) + rows(0, -2) + rows(0, 2),
            )
            field_last[c, e] = 2.0 * here - middle[c, e] + speed_sq[e] * total
        last_copy(c).start()
        return carry

    lax.fori_loop(0, 3, second, 0)

    lane = lax.broadcasted_iota(jnp.int32, (1, CZ), 1)
    parts[...] = jnp.zeros_like(parts)
    for copy in subs:
        copy.wait()
    for i in range(SUBS):
        cell, patch = cells[i], patches[i]
        layer, row, depth = cell >> 12, (cell >> 7) & (CN - 1), cell & (CZ - 1)
        total = jnp.zeros((1, CZ), jnp.float32)
        for c in range(3):
            total += mechanism[c, i] * later[c, layer + 2, pl.ds(TOP + row, 1), :]
            total += mechanism[3 + c, i] * field_last[c, layer, pl.ds(row, 1), :]
        total = jnp.where(lane == depth, total, 0.0)
        run, at = patch >> 11, (patch >> 6) & (PLANE - 1)
        place = (at & (PER_ROW - 1)) * PATCH_DEV + (patch & (PATCH_DEV - 1))
        turned = pltpu.roll(total, (place - depth) & (CZ - 1), 1)
        to = run * N_NORTH + ((patch >> 3) & (N_NORTH - 1))
        parts[to, pl.ds(at >> 4, 1), :] += turned
    for c in range(3):
        next_copy(c).wait()
        last_copy(c).wait()


def spread_kernel(parts, out):
    total = jnp.sum(parts[...], axis=0)
    for row in range(ROWS):
        out[row * PER_ROW : (row + 1) * PER_ROW] = jnp.broadcast_to(
            total[row : row + 1][None], (PER_ROW, 1, CZ)
        )


def own_kernel(parts, out):
    total = jnp.sum(parts[...], axis=0)
    at = lax.axis_index("east") & (PER_ROW - 1)
    turned = pltpu.roll(total, (CZ - at * PATCH_DEV) & (CZ - 1), 1)
    out[...] = turned[:, 0:PATCH_DEV]


def body(field_prev, field_now, speed_sq, mechanism, sub_cells, sub_patch):
    params = pltpu.CompilerParams(vmem_limit_bytes=LIMIT)
    f32 = jnp.float32
    held = (
        pltpu.VMEM((3, CE, CN, CZ), f32), pltpu.VMEM((3, CE, CN, CZ), f32), pltpu.VMEM((CE, CN, CZ), f32)
    )
    east_message, north_message = pltpu.VMEM((E_LEN, CN, CZ), f32), pltpu.VMEM((N_LEN, CZ), f32)
    inputs = [pltpu.with_memory_space_constraint(x, pltpu.HBM) for x in (field_prev, field_now, speed_sq)]
    field_prev, field_now, speed_sq, far, near, low_pair, high_pair = pl.pallas_call(
        load_kernel, out_shape=[*held] + [north_message] * 2 + [east_message] * 2,
        in_specs=[HBM] * 3, out_specs=[VMEM] * 7,
        scratch_shapes=[pltpu.SemaphoreType.DMA((17,))], compiler_params=params, name="load",
    )(*inputs)
    far_pair = swap(far, "north", 1)
    near_pair = swap(near, "north", 0)
    pairs = swap(low_pair, "east", 0), swap(high_pair, "east", 1)
    low_corner, high_corner = pl.pallas_call(
        corner_kernel, out_shape=[pltpu.VMEM((C_LEN, CZ), f32)] * 2, in_specs=[VMEM] * 2,
        out_specs=[VMEM] * 2, compiler_params=params, name="corners",
    )(far_pair, near_pair)
    corners = swap(low_corner, "east", 0), swap(high_corner, "east", 1)
    wide = pltpu.VMEM((3, LAYERS, CN + 2 * TOP, CZ), f32)
    parts = pltpu.VMEM((COLUMN, ROWS, CZ), f32)
    field = pltpu.HBM((3, CE, CN, CZ), f32)
    subs = [pltpu.with_memory_space_constraint(x, pltpu.HBM) for x in (mechanism, sub_cells, sub_patch)]
    field_next, field_last, parts = pl.pallas_call(
        steps_kernel, out_shape=[field, field, parts], in_specs=[VMEM] * 9 + [HBM] * 3,
        out_specs=[HBM, HBM, VMEM],
        scratch_shapes=[
            wide, wide, pltpu.VMEM((3, CE, CN, CZ), f32),
            pltpu.VMEM((LAYERS, 16, CZ), f32), pltpu.VMEM((CE, 16, CZ), f32),
            pltpu.SMEM((6, SUBS), f32), pltpu.SMEM((SUBS,), jnp.int32), pltpu.SMEM((SUBS,), jnp.int32),
            pltpu.SemaphoreType.DMA((3,)), pltpu.SemaphoreType.DMA((6,)),
        ],
        compiler_params=params, name="steps",
    )(field_prev, field_now, speed_sq, far_pair, near_pair, *pairs, *corners, *subs)
    parts = lax.all_to_all(parts, BOTH, 0, 0, tiled=True, axis_index_groups=column_groups())
    parts = pl.pallas_call(
        spread_kernel, out_shape=jax.ShapeDtypeStruct((PLANE, 1, CZ), f32),
        in_specs=[VMEM], out_specs=VMEM, compiler_params=params, name="spread",
    )(parts)
    parts = lax.all_to_all(parts, BOTH, 0, 0, tiled=True, axis_index_groups=plane_groups())
    own = pl.pallas_call(
        own_kernel, out_shape=jax.ShapeDtypeStruct((1, PATCH_DEV), f32),
        in_specs=[VMEM], out_specs=VMEM, compiler_params=params, name="own",
    )(parts)
    return field_next, field_last, own.reshape(PATCH_DEV)


def solution(mesh):
    in_specs = (
        P(None, "east", "north", None),
        P(None, "east", "north", None),
        P("east", "north", None),
        P(None, BOTH),
        P(BOTH),
        P(BOTH),
    )
    out_specs = (
        P(None, "east", "north", None),
        P(None, "east", "north", None),
        P(BOTH),
    )
    return jax.shard_map(body, mesh=mesh, in_specs=in_specs, out_specs=out_specs, check_vma=False)
```

```python
import jax
import jax.numpy as jnp
from jax import lax
from jax.experimental import pallas as pl
from jax.experimental.pallas import tpu as pltpu
from jax.sharding import PartitionSpec as P

BOTH = ("east", "north")
CE, CN, CZ = 8, 32, 128
SUBS = 16
N_NORTH = 8
PLANE = 32
Z_RUN = 3
COLUMN = Z_RUN * N_NORTH
PATCH_DEV = 8
PER_ROW = CZ // PATCH_DEV
ROWS = PLANE // PER_ROW
VMEM = pl.BlockSpec(memory_space=pltpu.VMEM)
SMEM = pl.BlockSpec(memory_space=pltpu.SMEM)
HBM = pl.BlockSpec(memory_space=pltpu.HBM)
LIMIT = 32 * 1024 * 1024

E_PREV, E_SPEED, E_SUBS, E_LEN = 12, 18, 20, 21
N_PREV, N_SPEED, N_SUBS, N_LEN = 96, 144, 160, 168
S_LEN = 8
C_LEN = 24
TOP = 16
LAYERS = CE + 4
NEAR, FAR = 16.0 / 12.0, -1.0 / 12.0


def column_groups():
    return [
        [(run * PLANE + at) * N_NORTH + n for run in range(Z_RUN) for n in range(N_NORTH)]
        for at in range(PLANE)
    ]


def plane_groups():
    return [
        [(run * PLANE + at) * N_NORTH + n for at in range(PLANE)]
        for run in range(Z_RUN)
        for n in range(N_NORTH)
    ]


def swap(block, axis, first):
    pairs = [(i, i + 1) for i in range(first, lax.axis_size(axis) - 1, 2)]
    return lax.ppermute(block, axis, pairs + [(j, i) for i, j in pairs])


def load_kernel(
    before, middle, speed_sq, mechanism_far, cells_far, cells_row_far, patches_row_far,
    before_here, middle_here, speed_here, far, near, low_pair, high_pair,
    mechanism, cells, cells_row, patches_row, sems,
):
    odd = lax.axis_index("east") & 1
    copies = [
        (cells_far, cells), (cells_row_far, cells_row), (patches_row_far, patches_row),
        (mechanism_far, mechanism), (speed_sq, speed_here), (middle, middle_here), (before, before_here),
    ]
    first = len(copies)
    for message, high in ((low_pair, 1 - odd), (high_pair, odd)):
        four, two = high * (CE - 4), high * (CE - 2)
        for c in range(3):
            copies.append((middle.at[c, pl.ds(four, 4)], message.at[pl.ds(c * 4, 4)]))
            copies.append((before.at[c, pl.ds(two, 2)], message.at[pl.ds(E_PREV + c * 2, 2)]))
        copies.append((speed_sq.at[pl.ds(two, 2)], message.at[pl.ds(E_SPEED, 2)]))
    started = [pltpu.make_async_copy(a, b, sems.at[i]) for i, (a, b) in enumerate(copies)]
    for copy in started:
        copy.start()
    for copy in started[:first]:
        copy.wait()
    odd_north = (lax.axis_index("north") & 1) == 1

    def put(at, count, low, high):
        near[at : at + count, :] = jnp.where(odd_north, low, high)
        far[at : at + count, :] = jnp.where(odd_north, high, low)

    for e in range(CE):
        for c in range(3):
            slot = c * CE + e
            put(slot * 4, 4, middle_here[c, e, 0:4, :], middle_here[c, e, CN - 4 : CN, :])
            put(N_PREV + slot * 2, 2, before_here[c, e, 0:2, :], before_here[c, e, CN - 2 : CN, :])
        put(N_SPEED + e * 2, 2, speed_here[e, 0:2, :], speed_here[e, CN - 2 : CN, :])
    lane = lax.broadcasted_iota(jnp.int32, (1, CZ), 1)
    speeds = jnp.zeros((1, CZ), jnp.float32)
    for i in range(SUBS):
        cell = cells[i]
        depth = cell & (CZ - 1)
        row = speed_here[cell >> 12, pl.ds((cell >> 7) & (CN - 1), 1), :]
        speeds += pltpu.roll(jnp.where(lane == depth, row, 0.0), (i - depth) & (CZ - 1), 1)
    for message in (near, far):
        message[N_SUBS : N_SUBS + S_LEN, :] = jnp.zeros((S_LEN, CZ), jnp.float32)
        message[N_SUBS : N_SUBS + 1, 0:SUBS] = cells_row[...].astype(jnp.float32)
        message[N_SUBS + 1 : N_SUBS + 2, 0:SUBS] = patches_row[...].astype(jnp.float32)
        message[N_SUBS + 2 : N_SUBS + 5, 0:SUBS] = mechanism[3:6, :] * speeds[:, 0:SUBS]
    for message in (low_pair, high_pair):
        message[E_SUBS] = jnp.zeros((CN, CZ), jnp.float32)
        message[E_SUBS, 0:S_LEN, :] = near[N_SUBS : N_SUBS + S_LEN, :]
    for copy in started[first:]:
        copy.wait()


def east_layers(low_pair, high_pair):
    odd = (lax.axis_index("east") & 1) == 1

    def west(k):
        return jnp.where(odd, low_pair[k], high_pair[k])

    def east(k):
        return jnp.where(odd, high_pair[k], low_pair[k])

    return west, east


def north_rows(near_pair, far_pair):
    odd = (lax.axis_index("north") & 1) == 1

    def south(at, count):
        return jnp.where(odd, near_pair[pl.ds(at, count), :], far_pair[pl.ds(at, count), :])

    def north(at, count):
        return jnp.where(odd, far_pair[pl.ds(at, count), :], near_pair[pl.ds(at, count), :])

    return south, north


def put_corners(south, north, low_pair, high_pair):
    odd = (lax.axis_index("east") & 1) == 1
    for c in range(3):
        for k in range(2):
            at = (c * 2 + k) * 4
            low, high = (c * CE + k) * 4, (c * CE + CE - 2 + k) * 4
            for rows, lows, highs in (
                (slice(at, at + 2), south(low + 2, 2), south(high + 2, 2)),
                (slice(at + 2, at + 4), north(low, 2), north(high, 2)),
            ):
                low_pair[rows, :] = jnp.where(odd, lows, highs)
                high_pair[rows, :] = jnp.where(odd, highs, lows)


def laplace(here, near, far):
    lane = lax.broadcasted_iota(jnp.int32, here.shape, 1)
    near += jnp.where(lane >= 1, pltpu.roll(here, 1, 1), 0.0)
    near += jnp.where(lane < CZ - 1, pltpu.roll(here, CZ - 1, 1), 0.0)
    far += jnp.where(lane >= 2, pltpu.roll(here, 2, 1), 0.0)
    far += jnp.where(lane < CZ - 2, pltpu.roll(here, CZ - 2, 1), 0.0)
    return near * (16.0 / 12.0) - far * (1.0 / 12.0) - here * 7.5


def steps_kernel(
    before, middle, speed_sq, far_pair, near_pair, low_pair, high_pair,
    mechanism_far, cells_far, patches_far, next_out, field_last, parts, low_corner, high_corner,
    wide, later, beyond, edge_before, edge_speed, mechanism, cells, patches, theirs, sub_sems, out_sems,
):
    subs = [
        pltpu.make_async_copy(a, b, sub_sems.at[i])
        for i, (a, b) in enumerate(
            (
                (mechanism_far, mechanism), (cells_far, cells), (patches_far, patches),
                (low_pair.at[E_SUBS, pl.ds(0, S_LEN)], theirs.at[0]),
                (high_pair.at[E_SUBS, pl.ds(0, S_LEN)], theirs.at[1]),
                (near_pair.at[pl.ds(N_SUBS, S_LEN)], theirs.at[2]),
                (far_pair.at[pl.ds(N_SUBS, S_LEN)], theirs.at[3]),
            )
        )
    ]
    for copy in subs:
        copy.start()

    def next_copy(c):
        own = later.at[c, pl.ds(2, CE), pl.ds(TOP, CN)]
        return pltpu.make_async_copy(own, next_out.at[c], out_sems.at[c])


    west, east = east_layers(low_pair, high_pair)
    south, north = north_rows(near_pair, far_pair)
    put_corners(south, north, low_corner, high_corner)
    for e in range(CE):
        edge_speed[e, 6:8, :] = south(N_SPEED + e * 2, 2)
        edge_speed[e, 8:10, :] = north(N_SPEED + e * 2, 2)

    beyond[...] = jnp.zeros_like(beyond)

    def put_beyond(c):
        def row(layer, at):
            return wide[c, layer + 2, TOP + at : TOP + at + 1, :]

        def two(one, other):
            return NEAR * one + FAR * other, FAR * one

        def put(side, e, n, value):
            at = (e if e < 2 else e - 4) * 4 + (n if n < 2 else n - CN + 4)
            beyond[side, c, at : at + 1, :] = value

        for side, e, step in ((0, 0, 1), (1, CE - 1, -1)):
            mine = CE - 1 - e
            for n, inward, halo in ((0, 1, -1), (CN - 1, -1, CN)):
                sums = []
                for layer in (mine, mine - step):
                    near, far = two(row(layer, halo), row(layer, halo - inward))
                    sums.append((speed_sq[layer, n : n + 1, :] * near, speed_sq[layer, n + inward : n + inward + 1, :] * far))
                for j in range(2):
                    for i, value in enumerate(two(sums[0][j], sums[1][j])):
                        put(side, e + i * step, n + j * inward, value)
        for side, n, step in ((2, 0, 1), (3, CN - 1, -1)):
            mine = CN - 1 - n
            for e, inward, halo in ((0, 1, -1), (CE - 1, -1, CE)):
                sums = []
                for at in (mine, mine - step):
                    near, far = two(row(halo, at), row(halo - inward, at))
                    sums.append((speed_sq[e, at : at + 1, :] * near, speed_sq[e + inward, at : at + 1, :] * far))
                for i in range(2):
                    for j, value in enumerate(two(sums[0][i], sums[1][i])):
                        put(side, e + i * inward, n + j * step, value)

    def first(c, carry):
        def layer(k):
            if k < 0:
                return west(c * 4 + k + 4)
            if k >= CE:
                return east(c * 4 + k - CE)
            return middle[c, k]

        for e in range(-2, CE + 2):
            k = e + 2
            wide[c, k, TOP : TOP + CN, :] = layer(e)
            if 0 <= e < CE:
                at = pl.multiple_of((c * CE + e) * 4, 4)
                wide[c, k, TOP - 4 : TOP, :] = south(at, 4)
                wide[c, k, TOP + CN : TOP + CN + 4, :] = north(at, 4)
            else:
                wide[c, k, TOP - 2 : TOP, :] = jnp.zeros((2, CZ), jnp.float32)
                wide[c, k, TOP + CN : TOP + CN + 2, :] = jnp.zeros((2, CZ), jnp.float32)
        for e in range(-2, CE + 2):
            k = e + 2

            def rows(offset, count=CN):
                return wide[c, k, TOP + offset : TOP + offset + count, :]

            here = rows(0)
            total = laplace(
                here,
                layer(e - 1) + layer(e + 1) + rows(-1) + rows(1),
                layer(e - 2) + layer(e + 2) + rows(-2) + rows(2),
            )
            if 0 <= e < CE:
                old, speed = before[c, e], speed_sq[e]
            elif e < 0:
                old, speed = west(E_PREV + c * 2 + k), west(E_SPEED + k)
            else:
                old, speed = east(E_PREV + c * 2 + e - CE), east(E_SPEED + e - CE)
            new = 2.0 * here - old + speed * total
            later[c, k, TOP : TOP + CN, :] = new
        next_copy(c).start()
        put_beyond(c)
        for e in range(CE):
            k = e + 2
            at = pl.multiple_of(N_PREV + (c * CE + e) * 2, 2)
            edge_before[k, 6:8, :] = south(at, 2)
            edge_before[k, 8:10, :] = north(at, 2)
            for start, edge, kept in ((TOP - 8, 0, slice(6, 8)), (TOP + CN, 8, slice(0, 2))):

                def tile(layers, offset):
                    return wide[c, k + layers, start + offset : start + offset + 8, :]

                here = tile(0, 0)
                total = laplace(
                    here,
                    tile(-1, 0) + tile(1, 0) + tile(0, -1) + tile(0, 1),
                    tile(-2, 0) + tile(2, 0) + tile(0, -2) + tile(0, 2),
                )
                old, speed = edge_before[k, edge : edge + 8, :], edge_speed[e, edge : edge + 8, :]
                new = 2.0 * here - old + speed * total
                later[c, k, start + kept.start : start + kept.stop, :] = new[kept]
        return carry

    lax.fori_loop(0, 3, first, 0)

    def second(c, carry):
        for e in range(CE):
            k = e + 2

            def rows(layers, offset=0):
                return later[c, k + layers, TOP + offset : TOP + offset + CN, :]

            here = rows(0)
            total = laplace(
                here,
                rows(-1) + rows(1) + rows(0, -1) + rows(0, 1),
                rows(-2) + rows(2) + rows(0, -2) + rows(0, 2),
            )
            field_last[c, e] = 2.0 * here - middle[c, e] + speed_sq[e] * total
        return carry

    lax.fori_loop(0, 3, second, 0)

    lane = lax.broadcasted_iota(jnp.int32, (1, CZ), 1)
    parts[...] = jnp.zeros_like(parts)

    def add(total, depth, patch):
        run, at = patch >> 11, (patch >> 6) & (PLANE - 1)
        place = (at & (PER_ROW - 1)) * PATCH_DEV + (patch & (PATCH_DEV - 1))
        turned = pltpu.roll(jnp.where(lane == depth, total, 0.0), (place - depth) & (CZ - 1), 1)
        to = run * N_NORTH + ((patch >> 3) & (N_NORTH - 1))
        parts[to, pl.ds(at >> 4, 1), :] += turned

    for copy in subs:
        copy.wait()
    for i in range(SUBS):
        cell, patch = cells[i], patches[i]
        layer, row, depth = cell >> 12, (cell >> 7) & (CN - 1), cell & (CZ - 1)
        total = jnp.zeros((1, CZ), jnp.float32)
        for c in range(3):
            total += mechanism[c, i] * later[c, layer + 2, pl.ds(TOP + row, 1), :]
            total += mechanism[3 + c, i] * field_last[c, layer, pl.ds(row, 1), :]
        add(total, depth, patch)

    odd, odd_north = lax.axis_index("east") & 1, lax.axis_index("north") & 1
    sides = odd, 1 - odd, 2 + odd_north, 3 - odd_north

    def neighbours(i, carry):
        for m, side in enumerate(sides):
            cell = theirs[m, 0, i].astype(jnp.int32)
            layer, row, depth = cell >> 12, (cell >> 7) & (CN - 1), cell & (CZ - 1)

            @pl.when(((layer < 2) | (layer >= CE - 2)) & ((row < 2) | (row >= CN - 2)))
            def _():
                at = jnp.where(layer < 2, layer, layer - 4) * 4 + jnp.where(row < 2, row, row - CN + 4)
                total = jnp.zeros((1, CZ), jnp.float32)
                for c in range(3):
                    total += theirs[m, 2 + c, i] * beyond[side, c, pl.ds(at, 1), :]
                add(total, depth, theirs[m, 1, i].astype(jnp.int32))

        return carry

    lax.fori_loop(0, SUBS, neighbours, 0)
    for c in range(3):
        next_copy(c).wait()


def corner_kernel(
    last, speed_sq, far_pair, near_pair, low_pair, high_pair, low_corner, high_corner, out
):
    west, east = east_layers(low_pair, high_pair)
    south, north = north_rows(near_pair, far_pair)
    odd = (lax.axis_index("east") & 1) == 1
    low, high = low_corner[...], high_corner[...]
    weight = {1: NEAR, 2: FAR}
    out[...] = last[...]
    for column, corner, e0, e_step in (
        (west, jnp.where(odd, low, high), 0, 1), (east, jnp.where(odd, high, low), CE - 1, -1)
    ):
        columns = {i: column(E_SPEED + (2 - i if e0 == 0 else i - 1)) for i in (1, 2)}
        for rows, n0, n_step, first in ((south, 0, 1, 0), (north, CN - 1, -1, 2)):
            for e_in in range(2):
                e = e0 + e_in * e_step
                beside = rows(N_SPEED + e * 2, 2)
                for n_in in range(2):
                    n = n0 + n_in * n_step
                    for c in range(3):
                        total = jnp.zeros((1, CZ), jnp.float32)
                        for i in range(1, 3 - e_in):
                            k = 2 - i if e0 == 0 else i - 1
                            for j in range(1, 3 - n_in):
                                r = 2 - j if n0 == 0 else j - 1
                                at = (c * 2 + k) * 4 + first + r
                                speeds = columns[i][n : n + 1, :] + beside[r : r + 1, :]
                                total += (weight[e_in + i] * weight[n_in + j]) * corner[at : at + 1, :] * speeds
                        out[c, e, n : n + 1, :] += speed_sq[e, n : n + 1, :] * total


def spread_kernel(parts, _, out):
    total = jnp.sum(parts[...], axis=0)
    for row in range(ROWS):
        out[row * PER_ROW : (row + 1) * PER_ROW] = jnp.broadcast_to(
            total[row : row + 1][None], (PER_ROW, 1, CZ)
        )


def own_kernel(parts, out):
    total = jnp.sum(parts[...], axis=0)
    at = lax.axis_index("east") & (PER_ROW - 1)
    turned = pltpu.roll(total, (CZ - at * PATCH_DEV) & (CZ - 1), 1)
    out[...] = turned[:, 0:PATCH_DEV]


def body(field_prev, field_now, speed_sq, mechanism, sub_cells, sub_patch):
    params = pltpu.CompilerParams(vmem_limit_bytes=LIMIT)
    f32 = jnp.float32
    held = (
        pltpu.VMEM((3, CE, CN, CZ), f32), pltpu.VMEM((3, CE, CN, CZ), f32), pltpu.VMEM((CE, CN, CZ), f32)
    )
    east_message, north_message = pltpu.VMEM((E_LEN, CN, CZ), f32), pltpu.VMEM((N_LEN, CZ), f32)
    inputs = [
        pltpu.with_memory_space_constraint(x, pltpu.HBM)
        for x in (
            field_prev, field_now, speed_sq, mechanism, sub_cells,
            sub_cells.reshape(1, SUBS), sub_patch.reshape(1, SUBS), sub_patch,
        )
    ]
    i32 = jnp.int32
    field_prev, field_now, speed_sq, far, near, low_pair, high_pair = pl.pallas_call(
        load_kernel, out_shape=[*held] + [north_message] * 2 + [east_message] * 2,
        in_specs=[HBM] * 7, out_specs=[VMEM] * 7,
        scratch_shapes=[
            pltpu.VMEM((6, SUBS), f32), pltpu.SMEM((SUBS,), i32), pltpu.VMEM((1, SUBS), i32),
            pltpu.VMEM((1, SUBS), i32), pltpu.SemaphoreType.DMA((21,)),
        ],
        compiler_params=params, name="load",
    )(*inputs[:7])
    far_pair = swap(far, "north", 1)
    near_pair = swap(near, "north", 0)
    halos = far_pair, near_pair, swap(low_pair, "east", 0), swap(high_pair, "east", 1)
    wide = pltpu.VMEM((3, LAYERS, CN + 2 * TOP, CZ), f32)
    parts = pltpu.VMEM((COLUMN, ROWS, CZ), f32)
    corner = pltpu.VMEM((C_LEN, CZ), f32)
    field_next, field_last, parts, low_corner, high_corner = pl.pallas_call(
        steps_kernel,
        out_shape=[pltpu.HBM((3, CE, CN, CZ), f32), pltpu.VMEM((3, CE, CN, CZ), f32), parts, corner, corner],
        in_specs=[VMEM] * 7 + [HBM] * 3, out_specs=[HBM] + [VMEM] * 4,
        scratch_shapes=[
            wide, wide, pltpu.VMEM((4, 3, 16, CZ), f32),
            pltpu.VMEM((LAYERS, 16, CZ), f32), pltpu.VMEM((CE, 16, CZ), f32),
            pltpu.SMEM((6, SUBS), f32), pltpu.SMEM((SUBS,), i32), pltpu.SMEM((SUBS,), i32),
            pltpu.SMEM((4, S_LEN, CZ), f32),
            pltpu.SemaphoreType.DMA((7,)), pltpu.SemaphoreType.DMA((3,)),
        ],
        compiler_params=params, name="steps",
    )(field_prev, field_now, speed_sq, *halos, inputs[3], inputs[4], inputs[7])
    corners = swap(low_corner, "east", 0), swap(high_corner, "east", 1)
    parts = lax.all_to_all(parts, BOTH, 0, 0, tiled=True, axis_index_groups=column_groups())
    parts = pl.pallas_call(
        spread_kernel, out_shape=pltpu.VMEM((PLANE, 1, CZ), f32),
        in_specs=[VMEM] * 2, out_specs=VMEM, compiler_params=params, name="spread",
    )(parts, corners[0])
    parts = lax.all_to_all(parts, BOTH, 0, 0, tiled=True, axis_index_groups=plane_groups())
    own = pl.pallas_call(
        own_kernel, out_shape=jax.ShapeDtypeStruct((1, PATCH_DEV), f32),
        in_specs=[VMEM], out_specs=VMEM, compiler_params=params, name="own",
    )(parts)
    field_last = pl.pallas_call(
        corner_kernel, out_shape=jax.ShapeDtypeStruct((3, CE, CN, CZ), f32), in_specs=[VMEM] * 8,
        out_specs=VMEM, compiler_params=params, name="corners",
    )(field_last, speed_sq, *halos, *corners)
    return field_next, field_last, own.reshape(PATCH_DEV)


def solution(mesh):
    in_specs = (
        P(None, "east", "north", None),
        P(None, "east", "north", None),
        P("east", "north", None),
        P(None, BOTH),
        P(BOTH),
        P(BOTH),
    )
    out_specs = (
        P(None, "east", "north", None),
        P(None, "east", "north", None),
        P(BOTH),
    )
    return jax.shard_map(body, mesh=mesh, in_specs=in_specs, out_specs=out_specs, check_vma=False)
```

```python
import jax
import jax.numpy as jnp
from jax import lax
from jax.experimental import pallas as pl
from jax.experimental.pallas import tpu as pltpu
from jax.sharding import PartitionSpec as P

BOTH = ("east", "north")
CE, CN, CZ = 8, 32, 128
SUBS = 16
N_NORTH = 8
PLANE = 32
Z_RUN = 3
COLUMN = Z_RUN * N_NORTH
PATCH_DEV = 8
PER_ROW = CZ // PATCH_DEV
ROWS = PLANE // PER_ROW
VMEM = pl.BlockSpec(memory_space=pltpu.VMEM)
SMEM = pl.BlockSpec(memory_space=pltpu.SMEM)
HBM = pl.BlockSpec(memory_space=pltpu.HBM)
LIMIT = 32 * 1024 * 1024

E_PREV, E_SPEED, E_SUBS, E_LEN = 12, 18, 20, 21
N_PREV, N_SPEED, N_SUBS, N_LEN = 96, 144, 160, 168
S_LEN = 8
C_LEN = 24
TOP = 16
LAYERS = CE + 4
NEAR, FAR = 16.0 / 12.0, -1.0 / 12.0


def column_groups():
    return [
        [(run * PLANE + at) * N_NORTH + n for run in range(Z_RUN) for n in range(N_NORTH)]
        for at in range(PLANE)
    ]


def plane_groups():
    return [
        [(run * PLANE + at) * N_NORTH + n for at in range(PLANE)]
        for run in range(Z_RUN)
        for n in range(N_NORTH)
    ]


def swap(block, axis, first):
    pairs = [(i, i + 1) for i in range(first, lax.axis_size(axis) - 1, 2)]
    return lax.ppermute(block, axis, pairs + [(j, i) for i, j in pairs])


def load_kernel(
    before, middle, speed_sq, mechanism_far, cells_far, cells_row_far, patches_row_far,
    before_here, middle_here, speed_here, far, near, low_pair, high_pair,
    mechanism, cells, cells_row, patches_row, sems,
):
    odd = lax.axis_index("east") & 1
    copies = [
        (cells_far, cells), (cells_row_far, cells_row), (patches_row_far, patches_row),
        (mechanism_far, mechanism), (speed_sq, speed_here), (middle, middle_here), (before, before_here),
    ]
    first = len(copies)
    for message, high in ((low_pair, 1 - odd), (high_pair, odd)):
        four, two = high * (CE - 4), high * (CE - 2)
        for c in range(3):
            copies.append((middle.at[c, pl.ds(four, 4)], message.at[pl.ds(c * 4, 4)]))
            copies.append((before.at[c, pl.ds(two, 2)], message.at[pl.ds(E_PREV + c * 2, 2)]))
        copies.append((speed_sq.at[pl.ds(two, 2)], message.at[pl.ds(E_SPEED, 2)]))
    started = [pltpu.make_async_copy(a, b, sems.at[i]) for i, (a, b) in enumerate(copies)]
    for copy in started:
        copy.start()
    for copy in started[:first]:
        copy.wait()
    odd_north = (lax.axis_index("north") & 1) == 1

    def put(at, count, low, high):
        near[at : at + count, :] = jnp.where(odd_north, low, high)
        far[at : at + count, :] = jnp.where(odd_north, high, low)

    for e in range(CE):
        for c in range(3):
            slot = c * CE + e
            put(slot * 4, 4, middle_here[c, e, 0:4, :], middle_here[c, e, CN - 4 : CN, :])
            put(N_PREV + slot * 2, 2, before_here[c, e, 0:2, :], before_here[c, e, CN - 2 : CN, :])
        put(N_SPEED + e * 2, 2, speed_here[e, 0:2, :], speed_here[e, CN - 2 : CN, :])
    lane = lax.broadcasted_iota(jnp.int32, (1, CZ), 1)
    speeds = jnp.zeros((1, CZ), jnp.float32)
    for i in range(SUBS):
        cell = cells[i]
        depth = cell & (CZ - 1)
        row = speed_here[cell >> 12, pl.ds((cell >> 7) & (CN - 1), 1), :]
        speeds += pltpu.roll(jnp.where(lane == depth, row, 0.0), (i - depth) & (CZ - 1), 1)
    for message in (near, far):
        message[N_SUBS : N_SUBS + S_LEN, :] = jnp.zeros((S_LEN, CZ), jnp.float32)
        message[N_SUBS : N_SUBS + 1, 0:SUBS] = cells_row[...].astype(jnp.float32)
        message[N_SUBS + 1 : N_SUBS + 2, 0:SUBS] = patches_row[...].astype(jnp.float32)
        message[N_SUBS + 2 : N_SUBS + 5, 0:SUBS] = mechanism[3:6, :] * speeds[:, 0:SUBS]
    for message in (low_pair, high_pair):
        message[E_SUBS] = jnp.zeros((CN, CZ), jnp.float32)
        message[E_SUBS, 0:S_LEN, :] = near[N_SUBS : N_SUBS + S_LEN, :]
    for copy in started[first:]:
        copy.wait()


def east_layers(low_pair, high_pair):
    odd = (lax.axis_index("east") & 1) == 1

    def west(k):
        return jnp.where(odd, low_pair[k], high_pair[k])

    def east(k):
        return jnp.where(odd, high_pair[k], low_pair[k])

    return west, east


def north_rows(near_pair, far_pair):
    odd = (lax.axis_index("north") & 1) == 1

    def south(at, count):
        return jnp.where(odd, near_pair[pl.ds(at, count), :], far_pair[pl.ds(at, count), :])

    def north(at, count):
        return jnp.where(odd, far_pair[pl.ds(at, count), :], near_pair[pl.ds(at, count), :])

    return south, north


def put_corners(south, north, low_pair, high_pair):
    odd = (lax.axis_index("east") & 1) == 1
    for c in range(3):
        for k in range(2):
            at = (c * 2 + k) * 4
            low, high = (c * CE + k) * 4, (c * CE + CE - 2 + k) * 4
            for rows, lows, highs in (
                (slice(at, at + 2), south(low + 2, 2), south(high + 2, 2)),
                (slice(at + 2, at + 4), north(low, 2), north(high, 2)),
            ):
                low_pair[rows, :] = jnp.where(odd, lows, highs)
                high_pair[rows, :] = jnp.where(odd, highs, lows)


def laplace(here, near, far):
    lane = lax.broadcasted_iota(jnp.int32, here.shape, 1)
    near += jnp.where(lane >= 1, pltpu.roll(here, 1, 1), 0.0)
    near += jnp.where(lane < CZ - 1, pltpu.roll(here, CZ - 1, 1), 0.0)
    far += jnp.where(lane >= 2, pltpu.roll(here, 2, 1), 0.0)
    far += jnp.where(lane < CZ - 2, pltpu.roll(here, CZ - 2, 1), 0.0)
    return near * (16.0 / 12.0) - far * (1.0 / 12.0) - here * 7.5


def steps_kernel(
    before, middle, speed_sq, far_pair, near_pair, low_pair, high_pair,
    mechanism_far, cells_far, patches_far, next_out, later, parts, low_corner, high_corner,
    wide, beyond, edge_before, edge_speed, mechanism, cells, patches, theirs, sub_sems, out_sems,
):
    subs = [
        pltpu.make_async_copy(a, b, sub_sems.at[i])
        for i, (a, b) in enumerate(
            (
                (mechanism_far, mechanism), (cells_far, cells), (patches_far, patches),
                (low_pair.at[E_SUBS, pl.ds(0, S_LEN)], theirs.at[0]),
                (high_pair.at[E_SUBS, pl.ds(0, S_LEN)], theirs.at[1]),
                (near_pair.at[pl.ds(N_SUBS, S_LEN)], theirs.at[2]),
                (far_pair.at[pl.ds(N_SUBS, S_LEN)], theirs.at[3]),
            )
        )
    ]
    for copy in subs:
        copy.start()

    def next_copy(c):
        own = later.at[c, pl.ds(2, CE), pl.ds(TOP, CN)]
        return pltpu.make_async_copy(own, next_out.at[c], out_sems.at[c])


    west, east = east_layers(low_pair, high_pair)
    south, north = north_rows(near_pair, far_pair)
    put_corners(south, north, low_corner, high_corner)
    for e in range(CE):
        edge_speed[e, 6:8, :] = south(N_SPEED + e * 2, 2)
        edge_speed[e, 8:10, :] = north(N_SPEED + e * 2, 2)

    beyond[...] = jnp.zeros_like(beyond)

    def put_beyond(c):
        def row(layer, at):
            return wide[c, layer + 2, TOP + at : TOP + at + 1, :]

        def two(one, other):
            return NEAR * one + FAR * other, FAR * one

        def put(side, e, n, value):
            at = (e if e < 2 else e - 4) * 4 + (n if n < 2 else n - CN + 4)
            beyond[side, c, at : at + 1, :] = value

        for side, e, step in ((0, 0, 1), (1, CE - 1, -1)):
            mine = CE - 1 - e
            for n, inward, halo in ((0, 1, -1), (CN - 1, -1, CN)):
                sums = []
                for layer in (mine, mine - step):
                    near, far = two(row(layer, halo), row(layer, halo - inward))
                    sums.append((speed_sq[layer, n : n + 1, :] * near, speed_sq[layer, n + inward : n + inward + 1, :] * far))
                for j in range(2):
                    for i, value in enumerate(two(sums[0][j], sums[1][j])):
                        put(side, e + i * step, n + j * inward, value)
        for side, n, step in ((2, 0, 1), (3, CN - 1, -1)):
            mine = CN - 1 - n
            for e, inward, halo in ((0, 1, -1), (CE - 1, -1, CE)):
                sums = []
                for at in (mine, mine - step):
                    near, far = two(row(halo, at), row(halo - inward, at))
                    sums.append((speed_sq[e, at : at + 1, :] * near, speed_sq[e + inward, at : at + 1, :] * far))
                for i in range(2):
                    for j, value in enumerate(two(sums[0][i], sums[1][i])):
                        put(side, e + i * inward, n + j * step, value)

    def first(c, carry):
        def layer(k):
            if k < 0:
                return west(c * 4 + k + 4)
            if k >= CE:
                return east(c * 4 + k - CE)
            return middle[c, k]

        for e in range(-2, CE + 2):
            k = e + 2
            wide[c, k, TOP : TOP + CN, :] = layer(e)
            if 0 <= e < CE:
                at = pl.multiple_of((c * CE + e) * 4, 4)
                wide[c, k, TOP - 4 : TOP, :] = south(at, 4)
                wide[c, k, TOP + CN : TOP + CN + 4, :] = north(at, 4)
            else:
                wide[c, k, TOP - 2 : TOP, :] = jnp.zeros((2, CZ), jnp.float32)
                wide[c, k, TOP + CN : TOP + CN + 2, :] = jnp.zeros((2, CZ), jnp.float32)
        for e in range(-2, CE + 2):
            k = e + 2

            def rows(offset, count=CN):
                return wide[c, k, TOP + offset : TOP + offset + count, :]

            here = rows(0)
            total = laplace(
                here,
                layer(e - 1) + layer(e + 1) + rows(-1) + rows(1),
                layer(e - 2) + layer(e + 2) + rows(-2) + rows(2),
            )
            if 0 <= e < CE:
                old, speed = before[c, e], speed_sq[e]
            elif e < 0:
                old, speed = west(E_PREV + c * 2 + k), west(E_SPEED + k)
            else:
                old, speed = east(E_PREV + c * 2 + e - CE), east(E_SPEED + e - CE)
            new = 2.0 * here - old + speed * total
            later[c, k, TOP : TOP + CN, :] = new
        next_copy(c).start()
        put_beyond(c)
        for e in range(CE):
            k = e + 2
            at = pl.multiple_of(N_PREV + (c * CE + e) * 2, 2)
            edge_before[k, 6:8, :] = south(at, 2)
            edge_before[k, 8:10, :] = north(at, 2)
            for start, edge, kept in ((TOP - 8, 0, slice(6, 8)), (TOP + CN, 8, slice(0, 2))):

                def tile(layers, offset):
                    return wide[c, k + layers, start + offset : start + offset + 8, :]

                here = tile(0, 0)
                total = laplace(
                    here,
                    tile(-1, 0) + tile(1, 0) + tile(0, -1) + tile(0, 1),
                    tile(-2, 0) + tile(2, 0) + tile(0, -2) + tile(0, 2),
                )
                old, speed = edge_before[k, edge : edge + 8, :], edge_speed[e, edge : edge + 8, :]
                new = 2.0 * here - old + speed * total
                later[c, k, start + kept.start : start + kept.stop, :] = new[kept]
        return carry

    lax.fori_loop(0, 3, first, 0)

    lane = lax.broadcasted_iota(jnp.int32, (1, CZ), 1)
    parts[...] = jnp.zeros_like(parts)

    def add(total, depth, patch):
        run, at = patch >> 11, (patch >> 6) & (PLANE - 1)
        place = (at & (PER_ROW - 1)) * PATCH_DEV + (patch & (PATCH_DEV - 1))
        turned = pltpu.roll(jnp.where(lane == depth, total, 0.0), (place - depth) & (CZ - 1), 1)
        to = run * N_NORTH + ((patch >> 3) & (N_NORTH - 1))
        parts[to, pl.ds(at >> 4, 1), :] += turned

    for copy in subs:
        copy.wait()
    for i in range(SUBS):
        cell, patch = cells[i], patches[i]
        layer, row, depth = cell >> 12, (cell >> 7) & (CN - 1), cell & (CZ - 1)
        total, here, near, far = (jnp.zeros((1, CZ), jnp.float32) for _ in range(4))
        for c in range(3):

            def point(layers=0, rows=0):
                return later[c, layer + 2 + layers, pl.ds(TOP + row + rows, 1), :]

            weight = mechanism[3 + c, i]
            total += mechanism[c, i] * point() - weight * middle[c, layer, pl.ds(row, 1), :]
            here += weight * point()
            near += weight * (point(-1) + point(1) + point(0, -1) + point(0, 1))
            far += weight * (point(-2) + point(2) + point(0, -2) + point(0, 2))
        total += 2.0 * here + speed_sq[layer, pl.ds(row, 1), :] * laplace(here, near, far)
        add(total, depth, patch)

    odd, odd_north = lax.axis_index("east") & 1, lax.axis_index("north") & 1
    sides = odd, 1 - odd, 2 + odd_north, 3 - odd_north

    def neighbours(i, carry):
        for m, side in enumerate(sides):
            cell = theirs[m, 0, i].astype(jnp.int32)
            layer, row, depth = cell >> 12, (cell >> 7) & (CN - 1), cell & (CZ - 1)

            @pl.when(((layer < 2) | (layer >= CE - 2)) & ((row < 2) | (row >= CN - 2)))
            def _():
                at = jnp.where(layer < 2, layer, layer - 4) * 4 + jnp.where(row < 2, row, row - CN + 4)
                total = jnp.zeros((1, CZ), jnp.float32)
                for c in range(3):
                    total += theirs[m, 2 + c, i] * beyond[side, c, pl.ds(at, 1), :]
                add(total, depth, theirs[m, 1, i].astype(jnp.int32))

        return carry

    lax.fori_loop(0, SUBS, neighbours, 0)
    for c in range(3):
        next_copy(c).wait()


def last_kernel(middle, speed_sq, later, out):
    def component(c, carry):
        for e in range(CE):

            def rows(layers, offset=0):
                return later[c, e + 2 + layers, TOP + offset : TOP + offset + CN, :]

            here = rows(0)
            total = laplace(
                here,
                rows(-1) + rows(1) + rows(0, -1) + rows(0, 1),
                rows(-2) + rows(2) + rows(0, -2) + rows(0, 2),
            )
            out[c, e] = 2.0 * here - middle[c, e] + speed_sq[e] * total
        return carry

    lax.fori_loop(0, 3, component, 0)


def corner_kernel(
    last, speed_sq, far_pair, near_pair, low_pair, high_pair, low_corner, high_corner, out
):
    west, east = east_layers(low_pair, high_pair)
    south, north = north_rows(near_pair, far_pair)
    odd = (lax.axis_index("east") & 1) == 1
    low, high = low_corner[...], high_corner[...]
    weight = {1: NEAR, 2: FAR}
    out[...] = last[...]
    for column, corner, e0, e_step in (
        (west, jnp.where(odd, low, high), 0, 1), (east, jnp.where(odd, high, low), CE - 1, -1)
    ):
        columns = {i: column(E_SPEED + (2 - i if e0 == 0 else i - 1)) for i in (1, 2)}
        for rows, n0, n_step, first in ((south, 0, 1, 0), (north, CN - 1, -1, 2)):
            for e_in in range(2):
                e = e0 + e_in * e_step
                beside = rows(N_SPEED + e * 2, 2)
                for n_in in range(2):
                    n = n0 + n_in * n_step
                    for c in range(3):
                        total = jnp.zeros((1, CZ), jnp.float32)
                        for i in range(1, 3 - e_in):
                            k = 2 - i if e0 == 0 else i - 1
                            for j in range(1, 3 - n_in):
                                r = 2 - j if n0 == 0 else j - 1
                                at = (c * 2 + k) * 4 + first + r
                                speeds = columns[i][n : n + 1, :] + beside[r : r + 1, :]
                                total += (weight[e_in + i] * weight[n_in + j]) * corner[at : at + 1, :] * speeds
                        out[c, e, n : n + 1, :] += speed_sq[e, n : n + 1, :] * total


def spread_kernel(parts, _, out):
    total = jnp.sum(parts[...], axis=0)
    for row in range(ROWS):
        out[row * PER_ROW : (row + 1) * PER_ROW] = jnp.broadcast_to(
            total[row : row + 1][None], (PER_ROW, 1, CZ)
        )


def own_kernel(parts, out):
    total = jnp.sum(parts[...], axis=0)
    at = lax.axis_index("east") & (PER_ROW - 1)
    turned = pltpu.roll(total, (CZ - at * PATCH_DEV) & (CZ - 1), 1)
    out[...] = turned[:, 0:PATCH_DEV]


def body(field_prev, field_now, speed_sq, mechanism, sub_cells, sub_patch):
    params = pltpu.CompilerParams(vmem_limit_bytes=LIMIT)
    f32 = jnp.float32
    held = (
        pltpu.VMEM((3, CE, CN, CZ), f32), pltpu.VMEM((3, CE, CN, CZ), f32), pltpu.VMEM((CE, CN, CZ), f32)
    )
    east_message, north_message = pltpu.VMEM((E_LEN, CN, CZ), f32), pltpu.VMEM((N_LEN, CZ), f32)
    inputs = [
        pltpu.with_memory_space_constraint(x, pltpu.HBM)
        for x in (
            field_prev, field_now, speed_sq, mechanism, sub_cells,
            sub_cells.reshape(1, SUBS), sub_patch.reshape(1, SUBS), sub_patch,
        )
    ]
    i32 = jnp.int32
    field_prev, field_now, speed_sq, far, near, low_pair, high_pair = pl.pallas_call(
        load_kernel, out_shape=[*held] + [north_message] * 2 + [east_message] * 2,
        in_specs=[HBM] * 7, out_specs=[VMEM] * 7,
        scratch_shapes=[
            pltpu.VMEM((6, SUBS), f32), pltpu.SMEM((SUBS,), i32), pltpu.VMEM((1, SUBS), i32),
            pltpu.VMEM((1, SUBS), i32), pltpu.SemaphoreType.DMA((21,)),
        ],
        compiler_params=params, name="load",
    )(*inputs[:7])
    far_pair = swap(far, "north", 1)
    near_pair = swap(near, "north", 0)
    halos = far_pair, near_pair, swap(low_pair, "east", 0), swap(high_pair, "east", 1)
    wide = pltpu.VMEM((3, LAYERS, CN + 2 * TOP, CZ), f32)
    parts = pltpu.VMEM((COLUMN, ROWS, CZ), f32)
    corner = pltpu.VMEM((C_LEN, CZ), f32)
    field_next, later, parts, low_corner, high_corner = pl.pallas_call(
        steps_kernel,
        out_shape=[pltpu.HBM((3, CE, CN, CZ), f32), wide, parts, corner, corner],
        in_specs=[VMEM] * 7 + [HBM] * 3, out_specs=[HBM] + [VMEM] * 4,
        scratch_shapes=[
            wide, pltpu.VMEM((4, 3, 16, CZ), f32),
            pltpu.VMEM((LAYERS, 16, CZ), f32), pltpu.VMEM((CE, 16, CZ), f32),
            pltpu.SMEM((6, SUBS), f32), pltpu.SMEM((SUBS,), i32), pltpu.SMEM((SUBS,), i32),
            pltpu.SMEM((4, S_LEN, CZ), f32),
            pltpu.SemaphoreType.DMA((7,)), pltpu.SemaphoreType.DMA((3,)),
        ],
        compiler_params=params, name="steps",
    )(field_prev, field_now, speed_sq, *halos, inputs[3], inputs[4], inputs[7])
    corners = swap(low_corner, "east", 0), swap(high_corner, "east", 1)
    field_last = pl.pallas_call(
        last_kernel, out_shape=pltpu.VMEM((3, CE, CN, CZ), f32), in_specs=[VMEM] * 3, out_specs=VMEM,
        compiler_params=params, name="last",
        cost_estimate=pl.CostEstimate(flops=3_000_000, bytes_accessed=1_000_000, transcendentals=0),
    )(field_now, speed_sq, later)
    parts = lax.all_to_all(parts, BOTH, 0, 0, tiled=True, axis_index_groups=column_groups())
    parts = pl.pallas_call(
        spread_kernel, out_shape=pltpu.VMEM((PLANE, 1, CZ), f32),
        in_specs=[VMEM] * 2, out_specs=VMEM, compiler_params=params, name="spread",
    )(parts, corners[1])
    parts = lax.all_to_all(parts, BOTH, 0, 0, tiled=True, axis_index_groups=plane_groups())
    own = pl.pallas_call(
        own_kernel, out_shape=jax.ShapeDtypeStruct((1, PATCH_DEV), f32),
        in_specs=[VMEM], out_specs=VMEM, compiler_params=params, name="own",
    )(parts)
    field_last = pl.pallas_call(
        corner_kernel, out_shape=jax.ShapeDtypeStruct((3, CE, CN, CZ), f32), in_specs=[VMEM] * 8,
        out_specs=VMEM, compiler_params=params, name="corners",
    )(field_last, speed_sq, *halos, *corners)
    return field_next, field_last, own.reshape(PATCH_DEV)


def solution(mesh):
    in_specs = (
        P(None, "east", "north", None),
        P(None, "east", "north", None),
        P("east", "north", None),
        P(None, BOTH),
        P(BOTH),
        P(BOTH),
    )
    out_specs = (
        P(None, "east", "north", None),
        P(None, "east", "north", None),
        P(BOTH),
    )
    return jax.shard_map(body, mesh=mesh, in_specs=in_specs, out_specs=out_specs, check_vma=False)
```

```python
import jax
import jax.numpy as jnp
from jax import lax
from jax.experimental import pallas as pl
from jax.experimental.pallas import tpu as pltpu
from jax.sharding import PartitionSpec as P

BOTH = ("east", "north")
CE, CN, CZ = 8, 32, 128
SUBS = 16
N_NORTH = 8
PLANE = 32
Z_RUN = 3
COLUMN = Z_RUN * N_NORTH
PATCH_DEV = 8
PER_ROW = CZ // PATCH_DEV
ROWS = PLANE // PER_ROW
VMEM = pl.BlockSpec(memory_space=pltpu.VMEM)
SMEM = pl.BlockSpec(memory_space=pltpu.SMEM)
HBM = pl.BlockSpec(memory_space=pltpu.HBM)
LIMIT = 32 * 1024 * 1024

TILES = CN // 8
E_AHEAD, E_SPEED, E_SUBS = 6, 12, 14 * TILES
E_LEN = E_SUBS + 1
N_AHEAD, N_SPEED, N_SUBS, N_LEN = 48, 96, 112, 120
S_LEN = 8
C_LEN = 24
TOP = 16
LAYERS = CE + 4
NEAR, FAR = 16.0 / 12.0, -1.0 / 12.0


def column_groups():
    return [
        [(run * PLANE + at) * N_NORTH + n for run in range(Z_RUN) for n in range(N_NORTH)]
        for at in range(PLANE)
    ]


def plane_groups():
    return [
        [(run * PLANE + at) * N_NORTH + n for at in range(PLANE)]
        for run in range(Z_RUN)
        for n in range(N_NORTH)
    ]


def swap(block, axis, first):
    pairs = [(i, i + 1) for i in range(first, lax.axis_size(axis) - 1, 2)]
    return lax.ppermute(block, axis, pairs + [(j, i) for i, j in pairs])


def laplace(here, near, far):
    lane = lax.broadcasted_iota(jnp.int32, here.shape, 1)
    near += jnp.where(lane >= 1, pltpu.roll(here, 1, 1), 0.0)
    near += jnp.where(lane < CZ - 1, pltpu.roll(here, CZ - 1, 1), 0.0)
    far += jnp.where(lane >= 2, pltpu.roll(here, 2, 1), 0.0)
    far += jnp.where(lane < CZ - 2, pltpu.roll(here, CZ - 2, 1), 0.0)
    return near * NEAR + far * FAR - here * 7.5


def load_kernel(
    before_far, middle_far, speed_far, mechanism_far, cells_far, cells_row_far, patches_row_far,
    ahead, middle, speed_sq, far, near, low_pair, high_pair,
    before, wide, mechanism, cells, cells_row, patches_row, sems,
):
    copies = [
        (middle_far, middle), (before_far, before), (speed_far, speed_sq), (mechanism_far, mechanism),
        (cells_far, cells), (cells_row_far, cells_row), (patches_row_far, patches_row),
    ]
    started = [pltpu.make_async_copy(a, b, sems.at[i]) for i, (a, b) in enumerate(copies)]
    for copy in started:
        copy.start()
    odd = (lax.axis_index("east") & 1) == 1
    odd_north = (lax.axis_index("north") & 1) == 1
    for copy in started:
        copy.wait()

    def put_east(k, low, high):
        low, high = low.reshape(TILES, 8, CZ), high.reshape(TILES, 8, CZ)
        low_pair[pl.ds(k * TILES, TILES)] = jnp.where(odd, low, high)
        high_pair[pl.ds(k * TILES, TILES)] = jnp.where(odd, high, low)

    def put_north(at, field):
        low, high = field[0:2, :], field[CN - 2 : CN, :]
        near[pl.ds(at, 2), :] = jnp.where(odd_north, low, high)
        far[pl.ds(at, 2), :] = jnp.where(odd_north, high, low)

    def component(c, carry):
        for e in range(CE):
            here = middle[c, e]
            wide[e, 6:8, :] = jnp.zeros((2, CZ), jnp.float32)
            wide[e, 8 : 8 + CN, :] = here
            wide[e, 8 + CN : 10 + CN, :] = jnp.zeros((2, CZ), jnp.float32)

            def rows(offset):
                return wide[e, 8 + offset : 8 + offset + CN, :]

            near_sum, far_sum = rows(-1) + rows(1), rows(-2) + rows(2)
            for k in (e - 1, e + 1):
                near_sum += middle[c, k] if 0 <= k < CE else 0.0
            for k in (e - 2, e + 2):
                far_sum += middle[c, k] if 0 <= k < CE else 0.0
            total = 2.0 * here - before[c, e] + speed_sq[e] * laplace(here, near_sum, far_sum)
            ahead[c, e] = total
            at = pl.multiple_of((c * CE + e) * 2, 2)
            put_north(at, here)
            put_north(pl.multiple_of(N_AHEAD + at, 2), total)
        for k in range(2):
            put_east(c * 2 + k, middle[c, k], middle[c, CE - 2 + k])
            put_east(E_AHEAD + c * 2 + k, ahead[c, k], ahead[c, CE - 2 + k])
        return carry

    lax.fori_loop(0, 3, component, 0)
    for k in range(2):
        put_east(E_SPEED + k, speed_sq[k], speed_sq[CE - 2 + k])
    for e in range(CE):
        put_north(N_SPEED + e * 2, speed_sq[e])
    lane = lax.broadcasted_iota(jnp.int32, (1, CZ), 1)
    speeds = jnp.zeros((1, CZ), jnp.float32)
    for i in range(SUBS):
        cell = cells[i]
        depth = cell & (CZ - 1)
        row = speed_sq[cell >> 12, pl.ds((cell >> 7) & (CN - 1), 1), :]
        speeds += pltpu.roll(jnp.where(lane == depth, row, 0.0), (i - depth) & (CZ - 1), 1)
    near[N_SUBS : N_SUBS + S_LEN, :] = jnp.zeros((S_LEN, CZ), jnp.float32)
    near[N_SUBS : N_SUBS + 1, 0:SUBS] = cells_row[...].astype(jnp.float32)
    near[N_SUBS + 1 : N_SUBS + 2, 0:SUBS] = patches_row[...].astype(jnp.float32)
    near[N_SUBS + 2 : N_SUBS + 5, 0:SUBS] = mechanism[3:6, :] * speeds[:, 0:SUBS]
    subs = near[N_SUBS : N_SUBS + S_LEN, :]
    far[N_SUBS : N_SUBS + S_LEN, :] = subs
    low_pair[E_SUBS] = subs
    high_pair[E_SUBS] = subs


def east_layers(low_pair, high_pair):
    odd = (lax.axis_index("east") & 1) == 1

    def part(message, k, row):
        if row is None:
            return message[pl.ds(k * TILES, TILES)].reshape(CN, CZ)
        return message[k * TILES + row // 8, row % 8 : row % 8 + 1, :]

    def west(k, row=None):
        return jnp.where(odd, part(low_pair, k, row), part(high_pair, k, row))

    def east(k, row=None):
        return jnp.where(odd, part(high_pair, k, row), part(low_pair, k, row))

    return west, east


def north_rows(near_pair, far_pair):
    odd = (lax.axis_index("north") & 1) == 1

    def south(at, count):
        return jnp.where(odd, near_pair[pl.ds(at, count), :], far_pair[pl.ds(at, count), :])

    def north(at, count):
        return jnp.where(odd, far_pair[pl.ds(at, count), :], near_pair[pl.ds(at, count), :])

    return south, north


def put_corners(south, north, low_pair, high_pair):
    odd = (lax.axis_index("east") & 1) == 1
    for c in range(3):
        for k in range(2):
            at = (c * 2 + k) * 4
            low, high = (c * CE + k) * 2, (c * CE + CE - 2 + k) * 2
            for rows, lows, highs in (
                (slice(at, at + 2), south(low, 2), south(high, 2)),
                (slice(at + 2, at + 4), north(low, 2), north(high, 2)),
            ):
                low_pair[rows, :] = jnp.where(odd, lows, highs)
                high_pair[rows, :] = jnp.where(odd, highs, lows)


def steps_kernel(
    ahead, middle, speed_sq, far_pair, near_pair, low_pair, high_pair,
    mechanism_far, cells_far, patches_far, next_out, later, parts, low_corner, high_corner,
    beyond, mechanism, cells, patches, theirs, sub_sems, out_sems,
):
    subs = [
        pltpu.make_async_copy(a, b, sub_sems.at[i])
        for i, (a, b) in enumerate(
            (
                (mechanism_far, mechanism), (cells_far, cells), (patches_far, patches),
                (low_pair.at[E_SUBS], theirs.at[0]),
                (high_pair.at[E_SUBS], theirs.at[1]),
                (near_pair.at[pl.ds(N_SUBS, S_LEN)], theirs.at[2]),
                (far_pair.at[pl.ds(N_SUBS, S_LEN)], theirs.at[3]),
            )
        )
    ]
    for copy in subs:
        copy.start()

    def next_copy(c):
        own = later.at[c, pl.ds(2, CE), pl.ds(TOP, CN)]
        return pltpu.make_async_copy(own, next_out.at[c], out_sems.at[c])


    west, east = east_layers(low_pair, high_pair)
    south, north = north_rows(near_pair, far_pair)
    put_corners(south, north, low_corner, high_corner)
    beyond[...] = jnp.zeros_like(beyond)

    def put_beyond(c):
        def row(layer, at):
            if layer < 0:
                return west(c * 2 + layer + 2, at)
            if layer >= CE:
                return east(c * 2 + layer - CE, at)
            if at < 0:
                return south((c * CE + layer) * 2 + at + 2, 1)
            return north((c * CE + layer) * 2 + at - CN, 1)

        def two(one, other):
            return NEAR * one + FAR * other, FAR * one

        def put(side, e, n, value):
            at = (e if e < 2 else e - 4) * 4 + (n if n < 2 else n - CN + 4)
            beyond[side, c, at : at + 1, :] = value

        for side, e, step in ((0, 0, 1), (1, CE - 1, -1)):
            mine = CE - 1 - e
            for n, inward, halo in ((0, 1, -1), (CN - 1, -1, CN)):
                sums = []
                for layer in (mine, mine - step):
                    near, far = two(row(layer, halo), row(layer, halo - inward))
                    sums.append((speed_sq[layer, n : n + 1, :] * near, speed_sq[layer, n + inward : n + inward + 1, :] * far))
                for j in range(2):
                    for i, value in enumerate(two(sums[0][j], sums[1][j])):
                        put(side, e + i * step, n + j * inward, value)
        for side, n, step in ((2, 0, 1), (3, CN - 1, -1)):
            mine = CN - 1 - n
            for e, inward, halo in ((0, 1, -1), (CE - 1, -1, CE)):
                sums = []
                for at in (mine, mine - step):
                    near, far = two(row(halo, at), row(halo - inward, at))
                    sums.append((speed_sq[e, at : at + 1, :] * near, speed_sq[e + inward, at : at + 1, :] * far))
                for i in range(2):
                    for j, value in enumerate(two(sums[0][i], sums[1][i])):
                        put(side, e + i * inward, n + j * step, value)

    def first(c, carry):
        west_far, west_near = west(c * 2), west(c * 2 + 1)
        east_near, east_far = east(c * 2), east(c * 2 + 1)
        terms = {
            0: NEAR * west_near + FAR * west_far, 1: FAR * west_near,
            CE - 1: NEAR * east_near + FAR * east_far, CE - 2: FAR * east_near,
        }
        for e in range(CE):
            k = e + 2
            new = ahead[c, e]
            if e in terms:
                new += speed_sq[e] * terms[e]
            later[c, k, TOP : TOP + CN, :] = new
            at = (c * CE + e) * 2
            for take, n, step, one, two in ((south, 0, 1, 1, 0), (north, CN - 1, -1, 0, 1)):
                theirs_near, theirs_far = take(at + one, 1), take(at + two, 1)
                mine_near, mine_far = middle[c, e, n : n + 1, :], middle[c, e, n + step : n + step + 1, :]
                for row, extra in ((n, NEAR * theirs_near + FAR * theirs_far), (n + step, FAR * theirs_near)):
                    later[c, k, TOP + row : TOP + row + 1, :] += speed_sq[e, row : row + 1, :] * extra
                for row, part, extra in (
                    (n - step, one, NEAR * mine_near + FAR * mine_far), (n - 2 * step, two, FAR * mine_near)
                ):
                    later[c, k, TOP + row : TOP + row + 1, :] = (
                        take(N_AHEAD + at + part, 1) + take(N_SPEED + e * 2 + part, 1) * extra
                    )
        for k, take, part, extra in (
            (0, west, 0, FAR * middle[c, 0]), (1, west, 1, NEAR * middle[c, 0] + FAR * middle[c, 1]),
            (CE + 2, east, 0, NEAR * middle[c, CE - 1] + FAR * middle[c, CE - 2]),
            (CE + 3, east, 1, FAR * middle[c, CE - 1]),
        ):
            later[c, k, TOP : TOP + CN, :] = take(E_AHEAD + c * 2 + part) + take(E_SPEED + part) * extra
        next_copy(c).start()
        put_beyond(c)
        return carry

    lax.fori_loop(0, 3, first, 0)

    lane = lax.broadcasted_iota(jnp.int32, (1, CZ), 1)
    parts[...] = jnp.zeros_like(parts)

    def add(total, depth, patch):
        run, at = patch >> 11, (patch >> 6) & (PLANE - 1)
        place = (at & (PER_ROW - 1)) * PATCH_DEV + (patch & (PATCH_DEV - 1))
        turned = pltpu.roll(jnp.where(lane == depth, total, 0.0), (place - depth) & (CZ - 1), 1)
        to = run * N_NORTH + ((patch >> 3) & (N_NORTH - 1))
        parts[to, pl.ds(at >> 4, 1), :] += turned

    for copy in subs:
        copy.wait()
    for i in range(SUBS):
        cell, patch = cells[i], patches[i]
        layer, row, depth = cell >> 12, (cell >> 7) & (CN - 1), cell & (CZ - 1)
        total, here, near, far = (jnp.zeros((1, CZ), jnp.float32) for _ in range(4))
        for c in range(3):

            def point(layers=0, rows=0):
                return later[c, layer + 2 + layers, pl.ds(TOP + row + rows, 1), :]

            weight = mechanism[3 + c, i]
            total += mechanism[c, i] * point() - weight * middle[c, layer, pl.ds(row, 1), :]
            here += weight * point()
            near += weight * (point(-1) + point(1) + point(0, -1) + point(0, 1))
            far += weight * (point(-2) + point(2) + point(0, -2) + point(0, 2))
        total += 2.0 * here + speed_sq[layer, pl.ds(row, 1), :] * laplace(here, near, far)
        add(total, depth, patch)

    odd, odd_north = lax.axis_index("east") & 1, lax.axis_index("north") & 1
    sides = odd, 1 - odd, 2 + odd_north, 3 - odd_north

    def neighbours(i, carry):
        for m, side in enumerate(sides):
            cell = theirs[m, 0, i].astype(jnp.int32)
            layer, row, depth = cell >> 12, (cell >> 7) & (CN - 1), cell & (CZ - 1)

            @pl.when(((layer < 2) | (layer >= CE - 2)) & ((row < 2) | (row >= CN - 2)))
            def _():
                at = jnp.where(layer < 2, layer, layer - 4) * 4 + jnp.where(row < 2, row, row - CN + 4)
                total = jnp.zeros((1, CZ), jnp.float32)
                for c in range(3):
                    total += theirs[m, 2 + c, i] * beyond[side, c, pl.ds(at, 1), :]
                add(total, depth, theirs[m, 1, i].astype(jnp.int32))

        return carry

    lax.fori_loop(0, SUBS, neighbours, 0)
    for c in range(3):
        next_copy(c).wait()


def last_kernel(middle, speed_sq, later, out):
    def component(c, carry):
        for e in range(CE):

            def rows(layers, offset=0):
                return later[c, e + 2 + layers, TOP + offset : TOP + offset + CN, :]

            here = rows(0)
            total = laplace(
                here,
                rows(-1) + rows(1) + rows(0, -1) + rows(0, 1),
                rows(-2) + rows(2) + rows(0, -2) + rows(0, 2),
            )
            out[c, e] = 2.0 * here - middle[c, e] + speed_sq[e] * total
        return carry

    lax.fori_loop(0, 3, component, 0)


def corner_kernel(
    last, speed_sq, far_pair, near_pair, low_pair, high_pair, low_corner, high_corner, out
):
    west, east = east_layers(low_pair, high_pair)
    south, north = north_rows(near_pair, far_pair)
    odd = (lax.axis_index("east") & 1) == 1
    low, high = low_corner[...], high_corner[...]
    weight = {1: NEAR, 2: FAR}
    out[...] = last[...]
    for column, corner, e0, e_step in (
        (west, jnp.where(odd, low, high), 0, 1), (east, jnp.where(odd, high, low), CE - 1, -1)
    ):
        for rows, n0, n_step, first in ((south, 0, 1, 0), (north, CN - 1, -1, 2)):
            for e_in in range(2):
                e = e0 + e_in * e_step
                beside = rows(N_SPEED + e * 2, 2)
                for n_in in range(2):
                    n = n0 + n_in * n_step
                    for c in range(3):
                        total = jnp.zeros((1, CZ), jnp.float32)
                        for i in range(1, 3 - e_in):
                            k = 2 - i if e0 == 0 else i - 1
                            for j in range(1, 3 - n_in):
                                r = 2 - j if n0 == 0 else j - 1
                                at = (c * 2 + k) * 4 + first + r
                                speeds = column(E_SPEED + k, n) + beside[r : r + 1, :]
                                total += (weight[e_in + i] * weight[n_in + j]) * corner[at : at + 1, :] * speeds
                        out[c, e, n : n + 1, :] += speed_sq[e, n : n + 1, :] * total


def spread_kernel(parts, _, out):
    total = jnp.sum(parts[...], axis=0)
    for row in range(ROWS):
        out[row * PER_ROW : (row + 1) * PER_ROW] = jnp.broadcast_to(
            total[row : row + 1][None], (PER_ROW, 1, CZ)
        )


def own_kernel(parts, out):
    total = jnp.sum(parts[...], axis=0)
    at = lax.axis_index("east") & (PER_ROW - 1)
    turned = pltpu.roll(total, (CZ - at * PATCH_DEV) & (CZ - 1), 1)
    out[...] = turned[:, 0:PATCH_DEV]


def body(field_prev, field_now, speed_sq, mechanism, sub_cells, sub_patch):
    params = pltpu.CompilerParams(vmem_limit_bytes=LIMIT)
    f32 = jnp.float32
    field = pltpu.VMEM((3, CE, CN, CZ), f32)
    held = field, field, pltpu.VMEM((CE, CN, CZ), f32)
    east_message, north_message = pltpu.VMEM((E_LEN, 8, CZ), f32), pltpu.VMEM((N_LEN, CZ), f32)
    inputs = [
        pltpu.with_memory_space_constraint(x, pltpu.HBM)
        for x in (
            field_prev, field_now, speed_sq, mechanism, sub_cells,
            sub_cells.reshape(1, SUBS), sub_patch.reshape(1, SUBS), sub_patch,
        )
    ]
    i32 = jnp.int32
    ahead, field_now, speed_sq, far, near, low_pair, high_pair = pl.pallas_call(
        load_kernel, out_shape=[*held] + [north_message] * 2 + [east_message] * 2,
        in_specs=[HBM] * 7, out_specs=[VMEM] * 7,
        scratch_shapes=[
            field, pltpu.VMEM((CE, CN + 16, CZ), f32), pltpu.VMEM((6, SUBS), f32), pltpu.SMEM((SUBS,), i32),
            pltpu.VMEM((1, SUBS), i32), pltpu.VMEM((1, SUBS), i32), pltpu.SemaphoreType.DMA((7,)),
        ],
        compiler_params=params, name="load",
    )(*inputs[:7])
    far_pair = swap(far, "north", 1)
    near_pair = swap(near, "north", 0)
    halos = far_pair, near_pair, swap(low_pair, "east", 0), swap(high_pair, "east", 1)
    later = pltpu.VMEM((3, LAYERS, CN + 2 * TOP, CZ), f32)
    parts = pltpu.VMEM((COLUMN, ROWS, CZ), f32)
    corner = pltpu.VMEM((C_LEN, CZ), f32)
    field_next, later, parts, low_corner, high_corner = pl.pallas_call(
        steps_kernel,
        out_shape=[pltpu.HBM((3, CE, CN, CZ), f32), later, parts, corner, corner],
        in_specs=[VMEM] * 7 + [HBM] * 3, out_specs=[HBM] + [VMEM] * 4,
        scratch_shapes=[
            pltpu.VMEM((4, 3, 16, CZ), f32),
            pltpu.SMEM((6, SUBS), f32), pltpu.SMEM((SUBS,), i32), pltpu.SMEM((SUBS,), i32),
            pltpu.SMEM((4, S_LEN, CZ), f32),
            pltpu.SemaphoreType.DMA((7,)), pltpu.SemaphoreType.DMA((3,)),
        ],
        compiler_params=params, name="steps",
    )(ahead, field_now, speed_sq, *halos, inputs[3], inputs[4], inputs[7])
    corners = swap(low_corner, "east", 0), swap(high_corner, "east", 1)
    field_last = pl.pallas_call(
        last_kernel, out_shape=pltpu.VMEM((3, CE, CN, CZ), f32), in_specs=[VMEM] * 3, out_specs=VMEM,
        compiler_params=params, name="last",
        cost_estimate=pl.CostEstimate(flops=3_000_000, bytes_accessed=1_000_000, transcendentals=0),
    )(field_now, speed_sq, later)
    parts = lax.all_to_all(parts, BOTH, 0, 0, tiled=True, axis_index_groups=column_groups())
    parts = pl.pallas_call(
        spread_kernel, out_shape=pltpu.VMEM((PLANE, 1, CZ), f32),
        in_specs=[VMEM] * 2, out_specs=VMEM, compiler_params=params, name="spread",
    )(parts, corners[1])
    parts = lax.all_to_all(parts, BOTH, 0, 0, tiled=True, axis_index_groups=plane_groups())
    own = pl.pallas_call(
        own_kernel, out_shape=jax.ShapeDtypeStruct((1, PATCH_DEV), f32),
        in_specs=[VMEM], out_specs=VMEM, compiler_params=params, name="own",
    )(parts)
    field_last = pl.pallas_call(
        corner_kernel, out_shape=jax.ShapeDtypeStruct((3, CE, CN, CZ), f32), in_specs=[VMEM] * 8,
        out_specs=VMEM, compiler_params=params, name="corners",
    )(field_last, speed_sq, *halos, *corners)
    return field_next, field_last, own.reshape(PATCH_DEV)


def solution(mesh):
    in_specs = (
        P(None, "east", "north", None),
        P(None, "east", "north", None),
        P("east", "north", None),
        P(None, BOTH),
        P(BOTH),
        P(BOTH),
    )
    out_specs = (
        P(None, "east", "north", None),
        P(None, "east", "north", None),
        P(BOTH),
    )
    return jax.shard_map(body, mesh=mesh, in_specs=in_specs, out_specs=out_specs, check_vma=False)
```

```python
import jax
import jax.numpy as jnp
from jax import lax
from jax.experimental import pallas as pl
from jax.experimental.pallas import tpu as pltpu
from jax.sharding import PartitionSpec as P

BOTH = ("east", "north")
CE, CN, CZ = 8, 32, 128
SUBS = 16
N_NORTH = 8
PLANE = 32
Z_RUN = 3
COLUMN = Z_RUN * N_NORTH
PATCH_DEV = 8
PER_ROW = CZ // PATCH_DEV
ROWS = PLANE // PER_ROW
VMEM = pl.BlockSpec(memory_space=pltpu.VMEM)
SMEM = pl.BlockSpec(memory_space=pltpu.SMEM)
HBM = pl.BlockSpec(memory_space=pltpu.HBM)
LIMIT = 32 * 1024 * 1024

TILES = CN // 8
E_AHEAD, E_SPEED, E_SUBS = 6, 12, 14 * TILES
E_LEN = E_SUBS + 1
N_AHEAD, N_SPEED, N_SUBS, N_LEN = 48, 96, 112, 120
S_LEN = 8
C_LEN = 24
TOP = 16
LAYERS = CE + 4
NEAR, FAR = 16.0 / 12.0, -1.0 / 12.0


def column_groups():
    return [
        [(run * PLANE + at) * N_NORTH + n for run in range(Z_RUN) for n in range(N_NORTH)]
        for at in range(PLANE)
    ]


def plane_groups():
    return [
        [(run * PLANE + at) * N_NORTH + n for at in range(PLANE)]
        for run in range(Z_RUN)
        for n in range(N_NORTH)
    ]


def swap(block, axis, first):
    pairs = [(i, i + 1) for i in range(first, lax.axis_size(axis) - 1, 2)]
    return lax.ppermute(block, axis, pairs + [(j, i) for i, j in pairs])


def laplace(here, near, far):
    lane = lax.broadcasted_iota(jnp.int32, here.shape, 1)
    near += jnp.where(lane >= 1, pltpu.roll(here, 1, 1), 0.0)
    near += jnp.where(lane < CZ - 1, pltpu.roll(here, CZ - 1, 1), 0.0)
    far += jnp.where(lane >= 2, pltpu.roll(here, 2, 1), 0.0)
    far += jnp.where(lane < CZ - 2, pltpu.roll(here, CZ - 2, 1), 0.0)
    return near * NEAR + far * FAR - here * 7.5


def load_kernel(
    before_far, middle_far, speed_far, mechanism_far, cells_far, cells_row_far, patches_row_far,
    ahead, middle, speed_sq, far, near, low_pair, high_pair,
    before, wide, mechanism, cells, cells_row, patches_row, sems,
):
    copies = [
        (middle_far, middle), (before_far, before), (speed_far, speed_sq), (mechanism_far, mechanism),
        (cells_far, cells), (cells_row_far, cells_row), (patches_row_far, patches_row),
    ]
    started = [pltpu.make_async_copy(a, b, sems.at[i]) for i, (a, b) in enumerate(copies)]
    for copy in started:
        copy.start()
    odd = (lax.axis_index("east") & 1) == 1
    odd_north = (lax.axis_index("north") & 1) == 1
    for copy in started:
        copy.wait()

    def put_east(k, low, high):
        low, high = low.reshape(TILES, 8, CZ), high.reshape(TILES, 8, CZ)
        low_pair[pl.ds(k * TILES, TILES)] = jnp.where(odd, low, high)
        high_pair[pl.ds(k * TILES, TILES)] = jnp.where(odd, high, low)

    def put_north(at, field):
        low, high = field[0:2, :], field[CN - 2 : CN, :]
        near[pl.ds(at, 2), :] = jnp.where(odd_north, low, high)
        far[pl.ds(at, 2), :] = jnp.where(odd_north, high, low)

    def component(c, carry):
        for e in range(CE):
            here = middle[c, e]
            wide[e, 6:8, :] = jnp.zeros((2, CZ), jnp.float32)
            wide[e, 8 : 8 + CN, :] = here
            wide[e, 8 + CN : 10 + CN, :] = jnp.zeros((2, CZ), jnp.float32)

            def rows(offset):
                return wide[e, 8 + offset : 8 + offset + CN, :]

            near_sum, far_sum = rows(-1) + rows(1), rows(-2) + rows(2)
            for k in (e - 1, e + 1):
                near_sum += middle[c, k] if 0 <= k < CE else 0.0
            for k in (e - 2, e + 2):
                far_sum += middle[c, k] if 0 <= k < CE else 0.0
            total = 2.0 * here - before[c, e] + speed_sq[e] * laplace(here, near_sum, far_sum)
            ahead[c, e] = total
            at = pl.multiple_of((c * CE + e) * 2, 2)
            put_north(at, here)
            put_north(pl.multiple_of(N_AHEAD + at, 2), total)
        for k in range(2):
            put_east(c * 2 + k, middle[c, k], middle[c, CE - 2 + k])
            put_east(E_AHEAD + c * 2 + k, ahead[c, k], ahead[c, CE - 2 + k])
        return carry

    lax.fori_loop(0, 3, component, 0)
    for k in range(2):
        put_east(E_SPEED + k, speed_sq[k], speed_sq[CE - 2 + k])
    for e in range(CE):
        put_north(N_SPEED + e * 2, speed_sq[e])
    lane = lax.broadcasted_iota(jnp.int32, (1, CZ), 1)
    speeds = jnp.zeros((1, CZ), jnp.float32)
    for i in range(SUBS):
        cell = cells[i]
        depth = cell & (CZ - 1)
        row = speed_sq[cell >> 12, pl.ds((cell >> 7) & (CN - 1), 1), :]
        speeds += pltpu.roll(jnp.where(lane == depth, row, 0.0), (i - depth) & (CZ - 1), 1)
    near[N_SUBS : N_SUBS + S_LEN, :] = jnp.zeros((S_LEN, CZ), jnp.float32)
    near[N_SUBS : N_SUBS + 1, 0:SUBS] = cells_row[...].astype(jnp.float32)
    near[N_SUBS + 1 : N_SUBS + 2, 0:SUBS] = patches_row[...].astype(jnp.float32)
    near[N_SUBS + 2 : N_SUBS + 5, 0:SUBS] = mechanism[3:6, :] * speeds[:, 0:SUBS]
    subs = near[N_SUBS : N_SUBS + S_LEN, :]
    far[N_SUBS : N_SUBS + S_LEN, :] = subs
    low_pair[E_SUBS] = subs
    high_pair[E_SUBS] = subs


def east_layers(low_pair, high_pair):
    odd = (lax.axis_index("east") & 1) == 1

    def part(message, k, row):
        if row is None:
            return message[pl.ds(k * TILES, TILES)].reshape(CN, CZ)
        return message[k * TILES + row // 8, row % 8 : row % 8 + 1, :]

    def west(k, row=None):
        return jnp.where(odd, part(low_pair, k, row), part(high_pair, k, row))

    def east(k, row=None):
        return jnp.where(odd, part(high_pair, k, row), part(low_pair, k, row))

    return west, east


def north_rows(near_pair, far_pair):
    odd = (lax.axis_index("north") & 1) == 1

    def south(at, count):
        return jnp.where(odd, near_pair[pl.ds(at, count), :], far_pair[pl.ds(at, count), :])

    def north(at, count):
        return jnp.where(odd, far_pair[pl.ds(at, count), :], near_pair[pl.ds(at, count), :])

    return south, north


def put_corners(south, north, low_pair, high_pair):
    odd = (lax.axis_index("east") & 1) == 1
    for c in range(3):
        for k in range(2):
            at = (c * 2 + k) * 4
            low, high = (c * CE + k) * 2, (c * CE + CE - 2 + k) * 2
            for rows, lows, highs in (
                (slice(at, at + 2), south(low, 2), south(high, 2)),
                (slice(at + 2, at + 4), north(low, 2), north(high, 2)),
            ):
                low_pair[rows, :] = jnp.where(odd, lows, highs)
                high_pair[rows, :] = jnp.where(odd, highs, lows)


def steps_kernel(
    ahead, middle, speed_sq, far_pair, near_pair, low_pair, high_pair,
    mechanism_far, cells_far, patches_far, next_out, later, parts, low_corner, high_corner,
    beyond, mechanism, cells, patches, theirs, code_rows, codes, sub_sems, out_sems,
):
    subs = [
        pltpu.make_async_copy(a, b, sub_sems.at[i])
        for i, (a, b) in enumerate(
            (
                (mechanism_far, mechanism), (cells_far, cells), (patches_far, patches),
                (low_pair.at[E_SUBS], theirs.at[0]),
                (high_pair.at[E_SUBS], theirs.at[1]),
                (near_pair.at[pl.ds(N_SUBS, S_LEN)], theirs.at[2]),
                (far_pair.at[pl.ds(N_SUBS, S_LEN)], theirs.at[3]),
            )
        )
    ]
    for copy in subs:
        copy.start()
    for m, block in enumerate((low_pair[E_SUBS], high_pair[E_SUBS], near_pair[N_SUBS:N_LEN, :], far_pair[N_SUBS:N_LEN, :])):
        cell = block[0:1].astype(jnp.int32)
        layer, row = cell >> 12, (cell >> 7) & (CN - 1)
        corner = ((layer < 2) | (layer >= CE - 2)) & ((row < 2) | (row >= CN - 2))
        at = jnp.where(layer < 2, layer, layer - CE + 4) * 4 + jnp.where(row < 2, row, row - CN + 4)
        code_rows[2 * m : 2 * m + 1, :] = jnp.where(corner, at * CZ + (cell & (CZ - 1)), -1)
        code_rows[2 * m + 1 : 2 * m + 2, :] = block[1:2].astype(jnp.int32)
    coded = pltpu.make_async_copy(code_rows, codes, sub_sems.at[7])
    coded.start()

    def next_copy(c):
        own = later.at[c, pl.ds(2, CE), pl.ds(TOP, CN)]
        return pltpu.make_async_copy(own, next_out.at[c], out_sems.at[c])


    west, east = east_layers(low_pair, high_pair)
    south, north = north_rows(near_pair, far_pair)
    put_corners(south, north, low_corner, high_corner)
    beyond[...] = jnp.zeros_like(beyond)

    def put_beyond(c):
        def row(layer, at):
            if layer < 0:
                return west(c * 2 + layer + 2, at)
            if layer >= CE:
                return east(c * 2 + layer - CE, at)
            if at < 0:
                return south((c * CE + layer) * 2 + at + 2, 1)
            return north((c * CE + layer) * 2 + at - CN, 1)

        def two(one, other):
            return NEAR * one + FAR * other, FAR * one

        def put(side, e, n, value):
            at = (e if e < 2 else e - 4) * 4 + (n if n < 2 else n - CN + 4)
            beyond[side, c, at : at + 1, :] = value

        for side, e, step in ((0, 0, 1), (1, CE - 1, -1)):
            mine = CE - 1 - e
            for n, inward, halo in ((0, 1, -1), (CN - 1, -1, CN)):
                sums = []
                for layer in (mine, mine - step):
                    near, far = two(row(layer, halo), row(layer, halo - inward))
                    sums.append((speed_sq[layer, n : n + 1, :] * near, speed_sq[layer, n + inward : n + inward + 1, :] * far))
                for j in range(2):
                    for i, value in enumerate(two(sums[0][j], sums[1][j])):
                        put(side, e + i * step, n + j * inward, value)
        for side, n, step in ((2, 0, 1), (3, CN - 1, -1)):
            mine = CN - 1 - n
            for e, inward, halo in ((0, 1, -1), (CE - 1, -1, CE)):
                sums = []
                for at in (mine, mine - step):
                    near, far = two(row(halo, at), row(halo - inward, at))
                    sums.append((speed_sq[e, at : at + 1, :] * near, speed_sq[e + inward, at : at + 1, :] * far))
                for i in range(2):
                    for j, value in enumerate(two(sums[0][i], sums[1][i])):
                        put(side, e + i * inward, n + j * step, value)

    row_of_two = lax.broadcasted_iota(jnp.int32, (2, CZ), 0)
    first_row, second_row = (jnp.where(row_of_two == r, NEAR, 0.0) for r in range(2))

    def two_rows(block, mask):
        return FAR * block + mask * jnp.concatenate([block[1:2], block[0:1]], axis=0)

    def first(c, carry):
        west_far, west_near = west(c * 2), west(c * 2 + 1)
        east_near, east_far = east(c * 2), east(c * 2 + 1)
        terms = {
            0: NEAR * west_near + FAR * west_far, 1: FAR * west_near,
            CE - 1: NEAR * east_near + FAR * east_far, CE - 2: FAR * east_near,
        }
        for e in range(CE):
            k = e + 2
            new = ahead[c, e]
            if e in terms:
                new += speed_sq[e] * terms[e]
            later[c, k, TOP : TOP + CN, :] = new
            at = (c * CE + e) * 2
            for take, n, outside, own_mask, halo_mask in (
                (south, 0, -2, first_row, second_row), (north, CN - 2, CN, second_row, first_row)
            ):
                inside = slice(TOP + n, TOP + n + 2)
                later[c, k, inside, :] += speed_sq[e, n : n + 2, :] * two_rows(take(at, 2), own_mask)
                later[c, k, TOP + outside : TOP + outside + 2, :] = take(N_AHEAD + at, 2) + take(
                    N_SPEED + e * 2, 2
                ) * two_rows(middle[c, e, n : n + 2, :], halo_mask)
        for k, take, part, extra in (
            (0, west, 0, FAR * middle[c, 0]), (1, west, 1, NEAR * middle[c, 0] + FAR * middle[c, 1]),
            (CE + 2, east, 0, NEAR * middle[c, CE - 1] + FAR * middle[c, CE - 2]),
            (CE + 3, east, 1, FAR * middle[c, CE - 1]),
        ):
            later[c, k, TOP : TOP + CN, :] = take(E_AHEAD + c * 2 + part) + take(E_SPEED + part) * extra
        next_copy(c).start()
        put_beyond(c)
        return carry

    lax.fori_loop(0, 3, first, 0)

    lane = lax.broadcasted_iota(jnp.int32, (1, CZ), 1)
    parts[...] = jnp.zeros_like(parts)

    def add(total, depth, patch):
        run, at = patch >> 11, (patch >> 6) & (PLANE - 1)
        place = (at & (PER_ROW - 1)) * PATCH_DEV + (patch & (PATCH_DEV - 1))
        turned = pltpu.roll(jnp.where(lane == depth, total, 0.0), (place - depth) & (CZ - 1), 1)
        to = run * N_NORTH + ((patch >> 3) & (N_NORTH - 1))
        parts[to, pl.ds(at >> 4, 1), :] += turned

    for copy in subs:
        copy.wait()
    for i in range(SUBS):
        cell, patch = cells[i], patches[i]
        layer, row, depth = cell >> 12, (cell >> 7) & (CN - 1), cell & (CZ - 1)
        total, here, near, far = (jnp.zeros((1, CZ), jnp.float32) for _ in range(4))
        for c in range(3):

            def point(layers=0, rows=0):
                return later[c, layer + 2 + layers, pl.ds(TOP + row + rows, 1), :]

            weight = mechanism[3 + c, i]
            total += mechanism[c, i] * point() - weight * middle[c, layer, pl.ds(row, 1), :]
            here += weight * point()
            near += weight * (point(-1) + point(1) + point(0, -1) + point(0, 1))
            far += weight * (point(-2) + point(2) + point(0, -2) + point(0, 2))
        total += 2.0 * here + speed_sq[layer, pl.ds(row, 1), :] * laplace(here, near, far)
        add(total, depth, patch)

    odd, odd_north = lax.axis_index("east") & 1, lax.axis_index("north") & 1
    sides = odd, 1 - odd, 2 + odd_north, 3 - odd_north

    def neighbours(i, carry):
        for m, side in enumerate(sides):
            code = codes[2 * m, i]

            @pl.when(code >= 0)
            def _():
                at, depth = code >> 7, code & (CZ - 1)
                total = jnp.zeros((1, CZ), jnp.float32)
                for c in range(3):
                    total += theirs[m, 2 + c, i] * beyond[side, c, pl.ds(at, 1), :]
                add(total, depth, codes[2 * m + 1, i])

        return carry

    coded.wait()
    lax.fori_loop(0, SUBS, neighbours, 0)
    for c in range(3):
        next_copy(c).wait()


def last_kernel(middle, speed_sq, later, out):
    def component(c, carry):
        for e in range(CE):

            def rows(layers, offset=0):
                return later[c, e + 2 + layers, TOP + offset : TOP + offset + CN, :]

            here = rows(0)
            total = laplace(
                here,
                rows(-1) + rows(1) + rows(0, -1) + rows(0, 1),
                rows(-2) + rows(2) + rows(0, -2) + rows(0, 2),
            )
            out[c, e] = 2.0 * here - middle[c, e] + speed_sq[e] * total
        return carry

    lax.fori_loop(0, 3, component, 0)


def corner_kernel(
    last, speed_sq, far_pair, near_pair, low_pair, high_pair, low_corner, high_corner, out
):
    west, east = east_layers(low_pair, high_pair)
    south, north = north_rows(near_pair, far_pair)
    odd = (lax.axis_index("east") & 1) == 1
    low, high = low_corner[...], high_corner[...]
    weight = {1: NEAR, 2: FAR}
    out[...] = last[...]
    for column, corner, e0, e_step in (
        (west, jnp.where(odd, low, high), 0, 1), (east, jnp.where(odd, high, low), CE - 1, -1)
    ):
        for rows, n0, n_step, first in ((south, 0, 1, 0), (north, CN - 1, -1, 2)):
            for e_in in range(2):
                e = e0 + e_in * e_step
                beside = rows(N_SPEED + e * 2, 2)
                for n_in in range(2):
                    n = n0 + n_in * n_step
                    for c in range(3):
                        total = jnp.zeros((1, CZ), jnp.float32)
                        for i in range(1, 3 - e_in):
                            k = 2 - i if e0 == 0 else i - 1
                            for j in range(1, 3 - n_in):
                                r = 2 - j if n0 == 0 else j - 1
                                at = (c * 2 + k) * 4 + first + r
                                speeds = column(E_SPEED + k, n) + beside[r : r + 1, :]
                                total += (weight[e_in + i] * weight[n_in + j]) * corner[at : at + 1, :] * speeds
                        out[c, e, n : n + 1, :] += speed_sq[e, n : n + 1, :] * total


def spread_kernel(parts, _, out):
    total = jnp.sum(parts[...], axis=0)
    for row in range(ROWS):
        out[row * PER_ROW : (row + 1) * PER_ROW] = jnp.broadcast_to(
            total[row : row + 1][None], (PER_ROW, 1, CZ)
        )


def own_kernel(parts, out):
    total = jnp.sum(parts[...], axis=0)
    at = lax.axis_index("east") & (PER_ROW - 1)
    turned = pltpu.roll(total, (CZ - at * PATCH_DEV) & (CZ - 1), 1)
    out[...] = turned[:, 0:PATCH_DEV]


def body(field_prev, field_now, speed_sq, mechanism, sub_cells, sub_patch):
    params = pltpu.CompilerParams(vmem_limit_bytes=LIMIT)
    f32 = jnp.float32
    field = pltpu.VMEM((3, CE, CN, CZ), f32)
    held = field, field, pltpu.VMEM((CE, CN, CZ), f32)
    east_message, north_message = pltpu.VMEM((E_LEN, 8, CZ), f32), pltpu.VMEM((N_LEN, CZ), f32)
    inputs = [
        pltpu.with_memory_space_constraint(x, pltpu.HBM)
        for x in (
            field_prev, field_now, speed_sq, mechanism, sub_cells,
            sub_cells.reshape(1, SUBS), sub_patch.reshape(1, SUBS), sub_patch,
        )
    ]
    i32 = jnp.int32
    ahead, field_now, speed_sq, far, near, low_pair, high_pair = pl.pallas_call(
        load_kernel, out_shape=[*held] + [north_message] * 2 + [east_message] * 2,
        in_specs=[HBM] * 7, out_specs=[VMEM] * 7,
        scratch_shapes=[
            field, pltpu.VMEM((CE, CN + 16, CZ), f32), pltpu.VMEM((6, SUBS), f32), pltpu.SMEM((SUBS,), i32),
            pltpu.VMEM((1, SUBS), i32), pltpu.VMEM((1, SUBS), i32), pltpu.SemaphoreType.DMA((7,)),
        ],
        compiler_params=params, name="load",
    )(*inputs[:7])
    far_pair = swap(far, "north", 1)
    near_pair = swap(near, "north", 0)
    halos = far_pair, near_pair, swap(low_pair, "east", 0), swap(high_pair, "east", 1)
    later = pltpu.VMEM((3, LAYERS, CN + 2 * TOP, CZ), f32)
    parts = pltpu.VMEM((COLUMN, ROWS, CZ), f32)
    corner = pltpu.VMEM((C_LEN, CZ), f32)
    field_next, later, parts, low_corner, high_corner = pl.pallas_call(
        steps_kernel,
        out_shape=[pltpu.HBM((3, CE, CN, CZ), f32), later, parts, corner, corner],
        in_specs=[VMEM] * 7 + [HBM] * 3, out_specs=[HBM] + [VMEM] * 4,
        scratch_shapes=[
            pltpu.VMEM((4, 3, 16, CZ), f32),
            pltpu.SMEM((6, SUBS), f32), pltpu.SMEM((SUBS,), i32), pltpu.SMEM((SUBS,), i32),
            pltpu.SMEM((4, S_LEN, CZ), f32), pltpu.VMEM((8, CZ), i32), pltpu.SMEM((8, CZ), i32),
            pltpu.SemaphoreType.DMA((8,)), pltpu.SemaphoreType.DMA((3,)),
        ],
        compiler_params=params, name="steps",
    )(ahead, field_now, speed_sq, *halos, inputs[3], inputs[4], inputs[7])
    corners = swap(low_corner, "east", 0), swap(high_corner, "east", 1)
    field_last = pl.pallas_call(
        last_kernel, out_shape=pltpu.VMEM((3, CE, CN, CZ), f32), in_specs=[VMEM] * 3, out_specs=VMEM,
        compiler_params=params, name="last",
        cost_estimate=pl.CostEstimate(flops=3_000_000, bytes_accessed=1_000_000, transcendentals=0),
    )(field_now, speed_sq, later)
    parts = lax.all_to_all(parts, BOTH, 0, 0, tiled=True, axis_index_groups=column_groups())
    parts = pl.pallas_call(
        spread_kernel, out_shape=pltpu.VMEM((PLANE, 1, CZ), f32),
        in_specs=[VMEM] * 2, out_specs=VMEM, compiler_params=params, name="spread",
    )(parts, corners[1])
    parts = lax.all_to_all(parts, BOTH, 0, 0, tiled=True, axis_index_groups=plane_groups())
    own = pl.pallas_call(
        own_kernel, out_shape=jax.ShapeDtypeStruct((1, PATCH_DEV), f32),
        in_specs=[VMEM], out_specs=VMEM, compiler_params=params, name="own",
    )(parts)
    field_last = pl.pallas_call(
        corner_kernel, out_shape=jax.ShapeDtypeStruct((3, CE, CN, CZ), f32), in_specs=[VMEM] * 8,
        out_specs=VMEM, compiler_params=params, name="corners",
    )(field_last, speed_sq, *halos, *corners)
    return field_next, field_last, own.reshape(PATCH_DEV)


def solution(mesh):
    in_specs = (
        P(None, "east", "north", None),
        P(None, "east", "north", None),
        P("east", "north", None),
        P(None, BOTH),
        P(BOTH),
        P(BOTH),
    )
    out_specs = (
        P(None, "east", "north", None),
        P(None, "east", "north", None),
        P(BOTH),
    )
    return jax.shard_map(body, mesh=mesh, in_specs=in_specs, out_specs=out_specs, check_vma=False)
```

```python
import jax
import jax.numpy as jnp
from jax import lax
from jax.experimental import pallas as pl
from jax.experimental.pallas import tpu as pltpu
from jax.sharding import PartitionSpec as P

BOTH = ("east", "north")
CE, CN, CZ = 8, 32, 128
SUBS = 16
N_NORTH = 8
PLANE = 32
Z_RUN = 3
COLUMN = Z_RUN * N_NORTH
PATCH_DEV = 8
PER_ROW = CZ // PATCH_DEV
ROWS = PLANE // PER_ROW
VMEM = pl.BlockSpec(memory_space=pltpu.VMEM)
SMEM = pl.BlockSpec(memory_space=pltpu.SMEM)
HBM = pl.BlockSpec(memory_space=pltpu.HBM)
LIMIT = 32 * 1024 * 1024

TILES = CN // 8
E_AHEAD, E_SPEED, E_SUBS = 6, 12, 14 * TILES
E_LEN = E_SUBS + 1
N_AHEAD, N_SPEED, N_SUBS, N_LEN = 48, 96, 112, 120
S_LEN = 8
C_LEN = 24
TOP = 16
LAYERS = CE + 4
NEAR, FAR = 16.0 / 12.0, -1.0 / 12.0


def column_groups():
    return [
        [(run * PLANE + at) * N_NORTH + n for run in range(Z_RUN) for n in range(N_NORTH)]
        for at in range(PLANE)
    ]


def plane_groups():
    return [
        [(run * PLANE + at) * N_NORTH + n for at in range(PLANE)]
        for run in range(Z_RUN)
        for n in range(N_NORTH)
    ]


def swap(block, axis, first):
    pairs = [(i, i + 1) for i in range(first, lax.axis_size(axis) - 1, 2)]
    return lax.ppermute(block, axis, pairs + [(j, i) for i, j in pairs])


def laplace(here, near, far):
    lane = lax.broadcasted_iota(jnp.int32, here.shape, 1)
    near += jnp.where(lane >= 1, pltpu.roll(here, 1, 1), 0.0)
    near += jnp.where(lane < CZ - 1, pltpu.roll(here, CZ - 1, 1), 0.0)
    far += jnp.where(lane >= 2, pltpu.roll(here, 2, 1), 0.0)
    far += jnp.where(lane < CZ - 2, pltpu.roll(here, CZ - 2, 1), 0.0)
    return near * NEAR + far * FAR - here * 7.5


def load_kernel(
    before_far, middle_far, speed_far, mechanism_far, cells_far, cells_row_far, patches_row_far,
    ahead, middle, speed_sq, far, near, low_pair, high_pair,
    before, wide, mechanism, cells, cells_row, patches_row, sems,
):
    def piece(c):
        return (
            pltpu.make_async_copy(middle_far.at[c], middle.at[c], sems.at[5 + c]),
            pltpu.make_async_copy(before_far.at[c], before.at[c], sems.at[8 + c]),
        )

    copies = [
        (speed_far, speed_sq), (mechanism_far, mechanism),
        (cells_far, cells), (cells_row_far, cells_row), (patches_row_far, patches_row),
    ]
    started = [pltpu.make_async_copy(a, b, sems.at[i]) for i, (a, b) in enumerate(copies)]
    started[0].start()
    for c in range(3):
        for copy in piece(c):
            copy.start()
    for copy in started[1:]:
        copy.start()
    odd = (lax.axis_index("east") & 1) == 1
    odd_north = (lax.axis_index("north") & 1) == 1
    started[0].wait()

    def put_east(k, low, high):
        low, high = low.reshape(TILES, 8, CZ), high.reshape(TILES, 8, CZ)
        low_pair[pl.ds(k * TILES, TILES)] = jnp.where(odd, low, high)
        high_pair[pl.ds(k * TILES, TILES)] = jnp.where(odd, high, low)

    def put_north(at, field):
        low, high = field[0:2, :], field[CN - 2 : CN, :]
        near[pl.ds(at, 2), :] = jnp.where(odd_north, low, high)
        far[pl.ds(at, 2), :] = jnp.where(odd_north, high, low)

    def component(c, carry):
        for copy in piece(c):
            copy.wait()
        for e in range(CE):
            here = middle[c, e]
            wide[e, 6:8, :] = jnp.zeros((2, CZ), jnp.float32)
            wide[e, 8 : 8 + CN, :] = here
            wide[e, 8 + CN : 10 + CN, :] = jnp.zeros((2, CZ), jnp.float32)

            def rows(offset):
                return wide[e, 8 + offset : 8 + offset + CN, :]

            near_sum, far_sum = rows(-1) + rows(1), rows(-2) + rows(2)
            for k in (e - 1, e + 1):
                near_sum += middle[c, k] if 0 <= k < CE else 0.0
            for k in (e - 2, e + 2):
                far_sum += middle[c, k] if 0 <= k < CE else 0.0
            total = 2.0 * here - before[c, e] + speed_sq[e] * laplace(here, near_sum, far_sum)
            ahead[c, e] = total
            at = pl.multiple_of((c * CE + e) * 2, 2)
            put_north(at, here)
            put_north(pl.multiple_of(N_AHEAD + at, 2), total)
        for k in range(2):
            put_east(c * 2 + k, middle[c, k], middle[c, CE - 2 + k])
            put_east(E_AHEAD + c * 2 + k, ahead[c, k], ahead[c, CE - 2 + k])
        return carry

    lax.fori_loop(0, 3, component, 0)
    for k in range(2):
        put_east(E_SPEED + k, speed_sq[k], speed_sq[CE - 2 + k])
    for e in range(CE):
        put_north(N_SPEED + e * 2, speed_sq[e])
    for copy in started[1:]:
        copy.wait()
    lane = lax.broadcasted_iota(jnp.int32, (1, CZ), 1)
    speeds = jnp.zeros((1, CZ), jnp.float32)
    for i in range(SUBS):
        cell = cells[i]
        depth = cell & (CZ - 1)
        row = speed_sq[cell >> 12, pl.ds((cell >> 7) & (CN - 1), 1), :]
        speeds += pltpu.roll(jnp.where(lane == depth, row, 0.0), (i - depth) & (CZ - 1), 1)
    near[N_SUBS : N_SUBS + S_LEN, :] = jnp.zeros((S_LEN, CZ), jnp.float32)
    near[N_SUBS : N_SUBS + 1, 0:SUBS] = cells_row[...].astype(jnp.float32)
    near[N_SUBS + 1 : N_SUBS + 2, 0:SUBS] = patches_row[...].astype(jnp.float32)
    near[N_SUBS + 2 : N_SUBS + 5, 0:SUBS] = mechanism[3:6, :] * speeds[:, 0:SUBS]
    subs = near[N_SUBS : N_SUBS + S_LEN, :]
    far[N_SUBS : N_SUBS + S_LEN, :] = subs
    low_pair[E_SUBS] = subs
    high_pair[E_SUBS] = subs


def east_layers(low_pair, high_pair):
    odd = (lax.axis_index("east") & 1) == 1

    def part(message, k, row):
        if row is None:
            return message[pl.ds(k * TILES, TILES)].reshape(CN, CZ)
        return message[k * TILES + row // 8, row % 8 : row % 8 + 1, :]

    def west(k, row=None):
        return jnp.where(odd, part(low_pair, k, row), part(high_pair, k, row))

    def east(k, row=None):
        return jnp.where(odd, part(high_pair, k, row), part(low_pair, k, row))

    return west, east


def north_rows(near_pair, far_pair):
    odd = (lax.axis_index("north") & 1) == 1

    def south(at, count):
        return jnp.where(odd, near_pair[pl.ds(at, count), :], far_pair[pl.ds(at, count), :])

    def north(at, count):
        return jnp.where(odd, far_pair[pl.ds(at, count), :], near_pair[pl.ds(at, count), :])

    return south, north


def put_corners(south, north, low_pair, high_pair):
    odd = (lax.axis_index("east") & 1) == 1
    for c in range(3):
        for k in range(2):
            at = (c * 2 + k) * 4
            low, high = (c * CE + k) * 2, (c * CE + CE - 2 + k) * 2
            for rows, lows, highs in (
                (slice(at, at + 2), south(low, 2), south(high, 2)),
                (slice(at + 2, at + 4), north(low, 2), north(high, 2)),
            ):
                low_pair[rows, :] = jnp.where(odd, lows, highs)
                high_pair[rows, :] = jnp.where(odd, highs, lows)


def steps_kernel(
    ahead, middle, speed_sq, far_pair, near_pair, low_pair, high_pair,
    mechanism_far, cells_far, patches_far, next_out, later, parts, low_corner, high_corner,
    beyond, mechanism, cells, patches, theirs, code_rows, codes, sub_sems, out_sems,
):
    subs = [
        pltpu.make_async_copy(a, b, sub_sems.at[i])
        for i, (a, b) in enumerate(
            (
                (mechanism_far, mechanism), (cells_far, cells), (patches_far, patches),
                (low_pair.at[E_SUBS], theirs.at[0]),
                (high_pair.at[E_SUBS], theirs.at[1]),
                (near_pair.at[pl.ds(N_SUBS, S_LEN)], theirs.at[2]),
                (far_pair.at[pl.ds(N_SUBS, S_LEN)], theirs.at[3]),
            )
        )
    ]
    for copy in subs:
        copy.start()
    for m, block in enumerate((low_pair[E_SUBS], high_pair[E_SUBS], near_pair[N_SUBS:N_LEN, :], far_pair[N_SUBS:N_LEN, :])):
        cell = block[0:1].astype(jnp.int32)
        layer, row = cell >> 12, (cell >> 7) & (CN - 1)
        corner = ((layer < 2) | (layer >= CE - 2)) & ((row < 2) | (row >= CN - 2))
        at = jnp.where(layer < 2, layer, layer - CE + 4) * 4 + jnp.where(row < 2, row, row - CN + 4)
        code_rows[2 * m : 2 * m + 1, :] = jnp.where(corner, at * CZ + (cell & (CZ - 1)), -1)
        code_rows[2 * m + 1 : 2 * m + 2, :] = block[1:2].astype(jnp.int32)
    coded = pltpu.make_async_copy(code_rows, codes, sub_sems.at[7])
    coded.start()

    def next_copy(c):
        own = later.at[c, pl.ds(2, CE), pl.ds(TOP, CN)]
        return pltpu.make_async_copy(own, next_out.at[c], out_sems.at[c])


    west, east = east_layers(low_pair, high_pair)
    south, north = north_rows(near_pair, far_pair)
    put_corners(south, north, low_corner, high_corner)
    beyond[...] = jnp.zeros_like(beyond)

    def put_beyond(c):
        def row(layer, at):
            if layer < 0:
                return west(c * 2 + layer + 2, at)
            if layer >= CE:
                return east(c * 2 + layer - CE, at)
            if at < 0:
                return south((c * CE + layer) * 2 + at + 2, 1)
            return north((c * CE + layer) * 2 + at - CN, 1)

        def two(one, other):
            return NEAR * one + FAR * other, FAR * one

        def put(side, e, n, value):
            at = (e if e < 2 else e - 4) * 4 + (n if n < 2 else n - CN + 4)
            beyond[side, c, at : at + 1, :] = value

        for side, e, step in ((0, 0, 1), (1, CE - 1, -1)):
            mine = CE - 1 - e
            for n, inward, halo in ((0, 1, -1), (CN - 1, -1, CN)):
                sums = []
                for layer in (mine, mine - step):
                    near, far = two(row(layer, halo), row(layer, halo - inward))
                    sums.append((speed_sq[layer, n : n + 1, :] * near, speed_sq[layer, n + inward : n + inward + 1, :] * far))
                for j in range(2):
                    for i, value in enumerate(two(sums[0][j], sums[1][j])):
                        put(side, e + i * step, n + j * inward, value)
        for side, n, step in ((2, 0, 1), (3, CN - 1, -1)):
            mine = CN - 1 - n
            for e, inward, halo in ((0, 1, -1), (CE - 1, -1, CE)):
                sums = []
                for at in (mine, mine - step):
                    near, far = two(row(halo, at), row(halo - inward, at))
                    sums.append((speed_sq[e, at : at + 1, :] * near, speed_sq[e + inward, at : at + 1, :] * far))
                for i in range(2):
                    for j, value in enumerate(two(sums[0][i], sums[1][i])):
                        put(side, e + i * inward, n + j * step, value)

    row_of_two = lax.broadcasted_iota(jnp.int32, (2, CZ), 0)
    first_row, second_row = (jnp.where(row_of_two == r, NEAR, 0.0) for r in range(2))

    def two_rows(block, mask):
        return FAR * block + mask * jnp.concatenate([block[1:2], block[0:1]], axis=0)

    def first(c, carry):
        west_far, west_near = west(c * 2), west(c * 2 + 1)
        east_near, east_far = east(c * 2), east(c * 2 + 1)
        terms = {
            0: NEAR * west_near + FAR * west_far, 1: FAR * west_near,
            CE - 1: NEAR * east_near + FAR * east_far, CE - 2: FAR * east_near,
        }
        for e in range(CE):
            k = e + 2
            new = ahead[c, e]
            if e in terms:
                new += speed_sq[e] * terms[e]
            later[c, k, TOP : TOP + CN, :] = new
            at = (c * CE + e) * 2
            for take, n, outside, own_mask, halo_mask in (
                (south, 0, -2, first_row, second_row), (north, CN - 2, CN, second_row, first_row)
            ):
                inside = slice(TOP + n, TOP + n + 2)
                later[c, k, inside, :] += speed_sq[e, n : n + 2, :] * two_rows(take(at, 2), own_mask)
                later[c, k, TOP + outside : TOP + outside + 2, :] = take(N_AHEAD + at, 2) + take(
                    N_SPEED + e * 2, 2
                ) * two_rows(middle[c, e, n : n + 2, :], halo_mask)
        for k, take, part, extra in (
            (0, west, 0, FAR * middle[c, 0]), (1, west, 1, NEAR * middle[c, 0] + FAR * middle[c, 1]),
            (CE + 2, east, 0, NEAR * middle[c, CE - 1] + FAR * middle[c, CE - 2]),
            (CE + 3, east, 1, FAR * middle[c, CE - 1]),
        ):
            later[c, k, TOP : TOP + CN, :] = take(E_AHEAD + c * 2 + part) + take(E_SPEED + part) * extra
        next_copy(c).start()
        put_beyond(c)
        return carry

    lax.fori_loop(0, 3, first, 0)

    lane = lax.broadcasted_iota(jnp.int32, (1, CZ), 1)
    parts[...] = jnp.zeros_like(parts)

    def add(total, depth, patch):
        run, at = patch >> 11, (patch >> 6) & (PLANE - 1)
        place = (at & (PER_ROW - 1)) * PATCH_DEV + (patch & (PATCH_DEV - 1))
        turned = pltpu.roll(jnp.where(lane == depth, total, 0.0), (place - depth) & (CZ - 1), 1)
        to = run * N_NORTH + ((patch >> 3) & (N_NORTH - 1))
        parts[to, pl.ds(at >> 4, 1), :] += turned

    for copy in subs:
        copy.wait()
    for i in range(SUBS):
        cell, patch = cells[i], patches[i]
        layer, row, depth = cell >> 12, (cell >> 7) & (CN - 1), cell & (CZ - 1)
        total, here, near, far = (jnp.zeros((1, CZ), jnp.float32) for _ in range(4))
        for c in range(3):

            def point(layers=0, rows=0):
                return later[c, layer + 2 + layers, pl.ds(TOP + row + rows, 1), :]

            weight = mechanism[3 + c, i]
            total += mechanism[c, i] * point() - weight * middle[c, layer, pl.ds(row, 1), :]
            here += weight * point()
            near += weight * (point(-1) + point(1) + point(0, -1) + point(0, 1))
            far += weight * (point(-2) + point(2) + point(0, -2) + point(0, 2))
        total += 2.0 * here + speed_sq[layer, pl.ds(row, 1), :] * laplace(here, near, far)
        add(total, depth, patch)

    odd, odd_north = lax.axis_index("east") & 1, lax.axis_index("north") & 1
    sides = odd, 1 - odd, 2 + odd_north, 3 - odd_north

    def neighbours(i, carry):
        for m, side in enumerate(sides):
            code = codes[2 * m, i]

            @pl.when(code >= 0)
            def _():
                at, depth = code >> 7, code & (CZ - 1)
                total = jnp.zeros((1, CZ), jnp.float32)
                for c in range(3):
                    total += theirs[m, 2 + c, i] * beyond[side, c, pl.ds(at, 1), :]
                add(total, depth, codes[2 * m + 1, i])

        return carry

    coded.wait()
    lax.fori_loop(0, SUBS, neighbours, 0)
    for c in range(3):
        next_copy(c).wait()


def last_kernel(middle, speed_sq, later, out):
    def component(c, carry):
        for e in range(CE):

            def rows(layers, offset=0):
                return later[c, e + 2 + layers, TOP + offset : TOP + offset + CN, :]

            here = rows(0)
            total = laplace(
                here,
                rows(-1) + rows(1) + rows(0, -1) + rows(0, 1),
                rows(-2) + rows(2) + rows(0, -2) + rows(0, 2),
            )
            out[c, e] = 2.0 * here - middle[c, e] + speed_sq[e] * total
        return carry

    lax.fori_loop(0, 3, component, 0)


def corner_kernel(
    last, speed_sq, far_pair, near_pair, low_pair, high_pair, low_corner, high_corner, out
):
    west, east = east_layers(low_pair, high_pair)
    south, north = north_rows(near_pair, far_pair)
    odd = (lax.axis_index("east") & 1) == 1
    low, high = low_corner[...], high_corner[...]
    weight = {1: NEAR, 2: FAR}
    out[...] = last[...]
    for column, corner, e0, e_step in (
        (west, jnp.where(odd, low, high), 0, 1), (east, jnp.where(odd, high, low), CE - 1, -1)
    ):
        for rows, n0, n_step, first in ((south, 0, 1, 0), (north, CN - 1, -1, 2)):
            for e_in in range(2):
                e = e0 + e_in * e_step
                beside = rows(N_SPEED + e * 2, 2)
                for n_in in range(2):
                    n = n0 + n_in * n_step
                    for c in range(3):
                        total = jnp.zeros((1, CZ), jnp.float32)
                        for i in range(1, 3 - e_in):
                            k = 2 - i if e0 == 0 else i - 1
                            for j in range(1, 3 - n_in):
                                r = 2 - j if n0 == 0 else j - 1
                                at = (c * 2 + k) * 4 + first + r
                                speeds = column(E_SPEED + k, n) + beside[r : r + 1, :]
                                total += (weight[e_in + i] * weight[n_in + j]) * corner[at : at + 1, :] * speeds
                        out[c, e, n : n + 1, :] += speed_sq[e, n : n + 1, :] * total


def spread_kernel(parts, _, out):
    total = jnp.sum(parts[...], axis=0)
    for row in range(ROWS):
        out[row * PER_ROW : (row + 1) * PER_ROW] = jnp.broadcast_to(
            total[row : row + 1][None], (PER_ROW, 1, CZ)
        )


def own_kernel(parts, out):
    total = jnp.sum(parts[...], axis=0)
    at = lax.axis_index("east") & (PER_ROW - 1)
    turned = pltpu.roll(total, (CZ - at * PATCH_DEV) & (CZ - 1), 1)
    out[...] = turned[:, 0:PATCH_DEV]


def body(field_prev, field_now, speed_sq, mechanism, sub_cells, sub_patch):
    params = pltpu.CompilerParams(vmem_limit_bytes=LIMIT)
    f32 = jnp.float32
    field = pltpu.VMEM((3, CE, CN, CZ), f32)
    held = field, field, pltpu.VMEM((CE, CN, CZ), f32)
    east_message, north_message = pltpu.VMEM((E_LEN, 8, CZ), f32), pltpu.VMEM((N_LEN, CZ), f32)
    inputs = [
        pltpu.with_memory_space_constraint(x, pltpu.HBM)
        for x in (
            field_prev, field_now, speed_sq, mechanism, sub_cells,
            sub_cells.reshape(1, SUBS), sub_patch.reshape(1, SUBS), sub_patch,
        )
    ]
    i32 = jnp.int32
    ahead, field_now, speed_sq, far, near, low_pair, high_pair = pl.pallas_call(
        load_kernel, out_shape=[*held] + [north_message] * 2 + [east_message] * 2,
        in_specs=[HBM] * 7, out_specs=[VMEM] * 7,
        scratch_shapes=[
            field, pltpu.VMEM((CE, CN + 16, CZ), f32), pltpu.VMEM((6, SUBS), f32), pltpu.SMEM((SUBS,), i32),
            pltpu.VMEM((1, SUBS), i32), pltpu.VMEM((1, SUBS), i32), pltpu.SemaphoreType.DMA((11,)),
        ],
        compiler_params=params, name="load",
    )(*inputs[:7])
    far_pair = swap(far, "north", 1)
    near_pair = swap(near, "north", 0)
    halos = far_pair, near_pair, swap(low_pair, "east", 0), swap(high_pair, "east", 1)
    later = pltpu.VMEM((3, LAYERS, CN + 2 * TOP, CZ), f32)
    parts = pltpu.VMEM((COLUMN, ROWS, CZ), f32)
    corner = pltpu.VMEM((C_LEN, CZ), f32)
    field_next, later, parts, low_corner, high_corner = pl.pallas_call(
        steps_kernel,
        out_shape=[pltpu.HBM((3, CE, CN, CZ), f32), later, parts, corner, corner],
        in_specs=[VMEM] * 7 + [HBM] * 3, out_specs=[HBM] + [VMEM] * 4,
        scratch_shapes=[
            pltpu.VMEM((4, 3, 16, CZ), f32),
            pltpu.SMEM((6, SUBS), f32), pltpu.SMEM((SUBS,), i32), pltpu.SMEM((SUBS,), i32),
            pltpu.SMEM((4, S_LEN, CZ), f32), pltpu.VMEM((8, CZ), i32), pltpu.SMEM((8, CZ), i32),
            pltpu.SemaphoreType.DMA((8,)), pltpu.SemaphoreType.DMA((3,)),
        ],
        compiler_params=params, name="steps",
    )(ahead, field_now, speed_sq, *halos, inputs[3], inputs[4], inputs[7])
    corners = swap(low_corner, "east", 0), swap(high_corner, "east", 1)
    field_last = pl.pallas_call(
        last_kernel, out_shape=pltpu.VMEM((3, CE, CN, CZ), f32), in_specs=[VMEM] * 3, out_specs=VMEM,
        compiler_params=params, name="last",
        cost_estimate=pl.CostEstimate(flops=3_000_000, bytes_accessed=1_000_000, transcendentals=0),
    )(field_now, speed_sq, later)
    parts = lax.all_to_all(parts, BOTH, 0, 0, tiled=True, axis_index_groups=column_groups())
    parts = pl.pallas_call(
        spread_kernel, out_shape=pltpu.VMEM((PLANE, 1, CZ), f32),
        in_specs=[VMEM] * 2, out_specs=VMEM, compiler_params=params, name="spread",
    )(parts, corners[1])
    parts = lax.all_to_all(parts, BOTH, 0, 0, tiled=True, axis_index_groups=plane_groups())
    own = pl.pallas_call(
        own_kernel, out_shape=jax.ShapeDtypeStruct((1, PATCH_DEV), f32),
        in_specs=[VMEM], out_specs=VMEM, compiler_params=params, name="own",
    )(parts)
    field_last = pl.pallas_call(
        corner_kernel, out_shape=jax.ShapeDtypeStruct((3, CE, CN, CZ), f32), in_specs=[VMEM] * 8,
        out_specs=VMEM, compiler_params=params, name="corners",
    )(field_last, speed_sq, *halos, *corners)
    return field_next, field_last, own.reshape(PATCH_DEV)


def solution(mesh):
    in_specs = (
        P(None, "east", "north", None),
        P(None, "east", "north", None),
        P("east", "north", None),
        P(None, BOTH),
        P(BOTH),
        P(BOTH),
    )
    out_specs = (
        P(None, "east", "north", None),
        P(None, "east", "north", None),
        P(BOTH),
    )
    return jax.shard_map(body, mesh=mesh, in_specs=in_specs, out_specs=out_specs, check_vma=False)
```

```python
import jax
import jax.numpy as jnp
from jax import lax
from jax.experimental import pallas as pl
from jax.experimental.pallas import tpu as pltpu
from jax.sharding import PartitionSpec as P

BOTH = ("east", "north")
CE, CN, CZ = 8, 32, 128
SUBS = 16
N_NORTH = 8
PLANE = 32
Z_RUN = 3
COLUMN = Z_RUN * N_NORTH
PATCH_DEV = 8
PER_ROW = CZ // PATCH_DEV
ROWS = PLANE // PER_ROW
VMEM = pl.BlockSpec(memory_space=pltpu.VMEM)
SMEM = pl.BlockSpec(memory_space=pltpu.SMEM)
HBM = pl.BlockSpec(memory_space=pltpu.HBM)
LIMIT = 32 * 1024 * 1024

TILES = CN // 8
E_AHEAD, E_SPEED, E_SUBS = 6, 12, 14 * TILES
E_LEN = E_SUBS + 1
N_AHEAD, N_SPEED, N_SUBS, N_LEN = 48, 96, 112, 120
S_LEN = 8
C_LEN = 24
TOP = 16
LAYERS = CE + 4
NEAR, FAR = 16.0 / 12.0, -1.0 / 12.0


def column_groups():
    return [
        [(run * PLANE + at) * N_NORTH + n for run in range(Z_RUN) for n in range(N_NORTH)]
        for at in range(PLANE)
    ]


def plane_groups():
    return [
        [(run * PLANE + at) * N_NORTH + n for at in range(PLANE)]
        for run in range(Z_RUN)
        for n in range(N_NORTH)
    ]


def swap(block, axis, first):
    pairs = [(i, i + 1) for i in range(first, lax.axis_size(axis) - 1, 2)]
    return lax.ppermute(block, axis, pairs + [(j, i) for i, j in pairs])


def laplace(here, near, far):
    lane = lax.broadcasted_iota(jnp.int32, here.shape, 1)
    near += jnp.where(lane >= 1, pltpu.roll(here, 1, 1), 0.0)
    near += jnp.where(lane < CZ - 1, pltpu.roll(here, CZ - 1, 1), 0.0)
    far += jnp.where(lane >= 2, pltpu.roll(here, 2, 1), 0.0)
    far += jnp.where(lane < CZ - 2, pltpu.roll(here, CZ - 2, 1), 0.0)
    return near * NEAR + far * FAR - here * 7.5


def load_kernel(
    before_far, middle_far, speed_far, mechanism_far, cells_far, cells_row_far, patches_row_far,
    ahead, middle, speed_sq, far, near, low_pair, high_pair,
    before, wide, mechanism, cells, cells_row, patches_row, sems,
):
    def piece(c):
        return (
            pltpu.make_async_copy(middle_far.at[c], middle.at[c], sems.at[5 + c]),
            pltpu.make_async_copy(before_far.at[c], before.at[c], sems.at[8 + c]),
        )

    copies = [
        (speed_far, speed_sq), (mechanism_far, mechanism),
        (cells_far, cells), (cells_row_far, cells_row), (patches_row_far, patches_row),
    ]
    started = [pltpu.make_async_copy(a, b, sems.at[i]) for i, (a, b) in enumerate(copies)]
    started[0].start()
    for c in range(3):
        for copy in piece(c):
            copy.start()
    for copy in started[1:]:
        copy.start()
    odd = (lax.axis_index("east") & 1) == 1
    odd_north = (lax.axis_index("north") & 1) == 1
    started[0].wait()

    def put_east(k, low, high):
        low, high = low.reshape(TILES, 8, CZ), high.reshape(TILES, 8, CZ)
        low_pair[pl.ds(k * TILES, TILES)] = jnp.where(odd, low, high)
        high_pair[pl.ds(k * TILES, TILES)] = jnp.where(odd, high, low)

    def put_north(at, field):
        low, high = field[0:2, :], field[CN - 2 : CN, :]
        near[pl.ds(at, 2), :] = jnp.where(odd_north, low, high)
        far[pl.ds(at, 2), :] = jnp.where(odd_north, high, low)

    def component(c, carry):
        for copy in piece(c):
            copy.wait()
        for e in range(CE):
            here = middle[c, e]
            wide[e, 6:8, :] = jnp.zeros((2, CZ), jnp.float32)
            wide[e, 8 : 8 + CN, :] = here
            wide[e, 8 + CN : 10 + CN, :] = jnp.zeros((2, CZ), jnp.float32)

            def rows(offset):
                return wide[e, 8 + offset : 8 + offset + CN, :]

            near_sum, far_sum = rows(-1) + rows(1), rows(-2) + rows(2)
            for k in (e - 1, e + 1):
                near_sum += middle[c, k] if 0 <= k < CE else 0.0
            for k in (e - 2, e + 2):
                far_sum += middle[c, k] if 0 <= k < CE else 0.0
            total = 2.0 * here - before[c, e] + speed_sq[e] * laplace(here, near_sum, far_sum)
            ahead[c, e] = total
            at = pl.multiple_of((c * CE + e) * 2, 2)
            put_north(at, here)
            put_north(pl.multiple_of(N_AHEAD + at, 2), total)
        for k in range(2):
            put_east(c * 2 + k, middle[c, k], middle[c, CE - 2 + k])
            put_east(E_AHEAD + c * 2 + k, ahead[c, k], ahead[c, CE - 2 + k])
        return carry

    lax.fori_loop(0, 3, component, 0)
    for k in range(2):
        put_east(E_SPEED + k, speed_sq[k], speed_sq[CE - 2 + k])
    for e in range(CE):
        put_north(N_SPEED + e * 2, speed_sq[e])
    for copy in started[1:]:
        copy.wait()
    lane = lax.broadcasted_iota(jnp.int32, (1, CZ), 1)
    speeds = jnp.zeros((1, CZ), jnp.float32)
    for i in range(SUBS):
        cell = cells[i]
        depth = cell & (CZ - 1)
        row = speed_sq[cell >> 12, pl.ds((cell >> 7) & (CN - 1), 1), :]
        speeds += pltpu.roll(jnp.where(lane == depth, row, 0.0), (i - depth) & (CZ - 1), 1)
    near[N_SUBS : N_SUBS + S_LEN, :] = jnp.zeros((S_LEN, CZ), jnp.float32)
    near[N_SUBS : N_SUBS + 1, 0:SUBS] = cells_row[...].astype(jnp.float32)
    near[N_SUBS + 1 : N_SUBS + 2, 0:SUBS] = patches_row[...].astype(jnp.float32)
    near[N_SUBS + 2 : N_SUBS + 5, 0:SUBS] = mechanism[3:6, :] * speeds[:, 0:SUBS]
    subs = near[N_SUBS : N_SUBS + S_LEN, :]
    far[N_SUBS : N_SUBS + S_LEN, :] = subs
    low_pair[E_SUBS] = subs
    high_pair[E_SUBS] = subs


def east_layers(low_pair, high_pair):
    odd = (lax.axis_index("east") & 1) == 1

    def part(message, k, row):
        if row is None:
            return message[pl.ds(k * TILES, TILES)].reshape(CN, CZ)
        return message[k * TILES + row // 8, row % 8 : row % 8 + 1, :]

    def west(k, row=None):
        return jnp.where(odd, part(low_pair, k, row), part(high_pair, k, row))

    def east(k, row=None):
        return jnp.where(odd, part(high_pair, k, row), part(low_pair, k, row))

    return west, east


def north_rows(near_pair, far_pair):
    odd = (lax.axis_index("north") & 1) == 1

    def south(at, count):
        return jnp.where(odd, near_pair[pl.ds(at, count), :], far_pair[pl.ds(at, count), :])

    def north(at, count):
        return jnp.where(odd, far_pair[pl.ds(at, count), :], near_pair[pl.ds(at, count), :])

    return south, north


def put_corners(south, north, low_pair, high_pair):
    odd = (lax.axis_index("east") & 1) == 1
    for c in range(3):
        for k in range(2):
            at = (c * 2 + k) * 4
            low, high = (c * CE + k) * 2, (c * CE + CE - 2 + k) * 2
            for rows, lows, highs in (
                (slice(at, at + 2), south(low, 2), south(high, 2)),
                (slice(at + 2, at + 4), north(low, 2), north(high, 2)),
            ):
                low_pair[rows, :] = jnp.where(odd, lows, highs)
                high_pair[rows, :] = jnp.where(odd, highs, lows)


def steps_kernel(
    ahead, middle, speed_sq, far_pair, near_pair, low_pair, high_pair,
    mechanism_far, cells_far, patches_far, next_out, later, parts,
    beyond, mechanism, cells, patches, theirs, code_rows, codes, sub_sems, out_sems,
):
    subs = [
        pltpu.make_async_copy(a, b, sub_sems.at[i])
        for i, (a, b) in enumerate(
            (
                (mechanism_far, mechanism), (cells_far, cells), (patches_far, patches),
                (low_pair.at[E_SUBS], theirs.at[0]),
                (high_pair.at[E_SUBS], theirs.at[1]),
                (near_pair.at[pl.ds(N_SUBS, S_LEN)], theirs.at[2]),
                (far_pair.at[pl.ds(N_SUBS, S_LEN)], theirs.at[3]),
            )
        )
    ]
    for copy in subs:
        copy.start()
    for m, block in enumerate((low_pair[E_SUBS], high_pair[E_SUBS], near_pair[N_SUBS:N_LEN, :], far_pair[N_SUBS:N_LEN, :])):
        cell = block[0:1].astype(jnp.int32)
        layer, row = cell >> 12, (cell >> 7) & (CN - 1)
        corner = ((layer < 2) | (layer >= CE - 2)) & ((row < 2) | (row >= CN - 2))
        at = jnp.where(layer < 2, layer, layer - CE + 4) * 4 + jnp.where(row < 2, row, row - CN + 4)
        code_rows[2 * m : 2 * m + 1, :] = jnp.where(corner, at * CZ + (cell & (CZ - 1)), -1)
        code_rows[2 * m + 1 : 2 * m + 2, :] = block[1:2].astype(jnp.int32)
    coded = pltpu.make_async_copy(code_rows, codes, sub_sems.at[7])
    coded.start()

    def next_copy(c):
        own = later.at[c, pl.ds(2, CE), pl.ds(TOP, CN)]
        return pltpu.make_async_copy(own, next_out.at[c], out_sems.at[c])


    west, east = east_layers(low_pair, high_pair)
    south, north = north_rows(near_pair, far_pair)
    beyond[...] = jnp.zeros_like(beyond)

    def put_beyond(c):
        def row(layer, at):
            if layer < 0:
                return west(c * 2 + layer + 2, at)
            if layer >= CE:
                return east(c * 2 + layer - CE, at)
            if at < 0:
                return south((c * CE + layer) * 2 + at + 2, 1)
            return north((c * CE + layer) * 2 + at - CN, 1)

        def two(one, other):
            return NEAR * one + FAR * other, FAR * one

        def put(side, e, n, value):
            at = (e if e < 2 else e - 4) * 4 + (n if n < 2 else n - CN + 4)
            beyond[side, c, at : at + 1, :] = value

        for side, e, step in ((0, 0, 1), (1, CE - 1, -1)):
            mine = CE - 1 - e
            for n, inward, halo in ((0, 1, -1), (CN - 1, -1, CN)):
                sums = []
                for layer in (mine, mine - step):
                    near, far = two(row(layer, halo), row(layer, halo - inward))
                    sums.append((speed_sq[layer, n : n + 1, :] * near, speed_sq[layer, n + inward : n + inward + 1, :] * far))
                for j in range(2):
                    for i, value in enumerate(two(sums[0][j], sums[1][j])):
                        put(side, e + i * step, n + j * inward, value)
        for side, n, step in ((2, 0, 1), (3, CN - 1, -1)):
            mine = CN - 1 - n
            for e, inward, halo in ((0, 1, -1), (CE - 1, -1, CE)):
                sums = []
                for at in (mine, mine - step):
                    near, far = two(row(halo, at), row(halo - inward, at))
                    sums.append((speed_sq[e, at : at + 1, :] * near, speed_sq[e + inward, at : at + 1, :] * far))
                for i in range(2):
                    for j, value in enumerate(two(sums[0][i], sums[1][i])):
                        put(side, e + i * inward, n + j * step, value)

    row_of_two = lax.broadcasted_iota(jnp.int32, (2, CZ), 0)
    first_row, second_row = (jnp.where(row_of_two == r, NEAR, 0.0) for r in range(2))

    def two_rows(block, mask):
        return FAR * block + mask * jnp.concatenate([block[1:2], block[0:1]], axis=0)

    def first(c, carry):
        west_far, west_near = west(c * 2), west(c * 2 + 1)
        east_near, east_far = east(c * 2), east(c * 2 + 1)
        terms = {
            0: NEAR * west_near + FAR * west_far, 1: FAR * west_near,
            CE - 1: NEAR * east_near + FAR * east_far, CE - 2: FAR * east_near,
        }
        for e in range(CE):
            k = e + 2
            new = ahead[c, e]
            if e in terms:
                new += speed_sq[e] * terms[e]
            later[c, k, TOP : TOP + CN, :] = new
            at = (c * CE + e) * 2
            for take, n, outside, own_mask, halo_mask in (
                (south, 0, -2, first_row, second_row), (north, CN - 2, CN, second_row, first_row)
            ):
                inside = slice(TOP + n, TOP + n + 2)
                later[c, k, inside, :] += speed_sq[e, n : n + 2, :] * two_rows(take(at, 2), own_mask)
                later[c, k, TOP + outside : TOP + outside + 2, :] = take(N_AHEAD + at, 2) + take(
                    N_SPEED + e * 2, 2
                ) * two_rows(middle[c, e, n : n + 2, :], halo_mask)
        for k, take, part, extra in (
            (0, west, 0, FAR * middle[c, 0]), (1, west, 1, NEAR * middle[c, 0] + FAR * middle[c, 1]),
            (CE + 2, east, 0, NEAR * middle[c, CE - 1] + FAR * middle[c, CE - 2]),
            (CE + 3, east, 1, FAR * middle[c, CE - 1]),
        ):
            later[c, k, TOP : TOP + CN, :] = take(E_AHEAD + c * 2 + part) + take(E_SPEED + part) * extra
        next_copy(c).start()
        put_beyond(c)
        return carry

    lax.fori_loop(0, 3, first, 0)

    lane = lax.broadcasted_iota(jnp.int32, (1, CZ), 1)
    parts[...] = jnp.zeros_like(parts)

    def add(total, depth, patch):
        run, at = patch >> 11, (patch >> 6) & (PLANE - 1)
        place = (at & (PER_ROW - 1)) * PATCH_DEV + (patch & (PATCH_DEV - 1))
        turned = pltpu.roll(jnp.where(lane == depth, total, 0.0), (place - depth) & (CZ - 1), 1)
        to = run * N_NORTH + ((patch >> 3) & (N_NORTH - 1))
        parts[to, pl.ds(at >> 4, 1), :] += turned

    for copy in subs:
        copy.wait()
    for i in range(SUBS):
        cell, patch = cells[i], patches[i]
        layer, row, depth = cell >> 12, (cell >> 7) & (CN - 1), cell & (CZ - 1)
        total, here, near, far = (jnp.zeros((1, CZ), jnp.float32) for _ in range(4))
        for c in range(3):

            def point(layers=0, rows=0):
                return later[c, layer + 2 + layers, pl.ds(TOP + row + rows, 1), :]

            weight = mechanism[3 + c, i]
            total += mechanism[c, i] * point() - weight * middle[c, layer, pl.ds(row, 1), :]
            here += weight * point()
            near += weight * (point(-1) + point(1) + point(0, -1) + point(0, 1))
            far += weight * (point(-2) + point(2) + point(0, -2) + point(0, 2))
        total += 2.0 * here + speed_sq[layer, pl.ds(row, 1), :] * laplace(here, near, far)
        add(total, depth, patch)

    odd, odd_north = lax.axis_index("east") & 1, lax.axis_index("north") & 1
    sides = odd, 1 - odd, 2 + odd_north, 3 - odd_north

    def neighbours(i, carry):
        for m, side in enumerate(sides):
            code = codes[2 * m, i]

            @pl.when(code >= 0)
            def _():
                at, depth = code >> 7, code & (CZ - 1)
                total = jnp.zeros((1, CZ), jnp.float32)
                for c in range(3):
                    total += theirs[m, 2 + c, i] * beyond[side, c, pl.ds(at, 1), :]
                add(total, depth, codes[2 * m + 1, i])

        return carry

    coded.wait()
    lax.fori_loop(0, SUBS, neighbours, 0)
    for c in range(3):
        next_copy(c).wait()


def corner_strips_kernel(far_pair, near_pair, _, low_corner, high_corner):
    put_corners(*north_rows(near_pair, far_pair), low_corner, high_corner)


def last_kernel(middle, speed_sq, later, out):
    def component(c, carry):
        for e in range(CE):

            def rows(layers, offset=0):
                return later[c, e + 2 + layers, TOP + offset : TOP + offset + CN, :]

            here = rows(0)
            total = laplace(
                here,
                rows(-1) + rows(1) + rows(0, -1) + rows(0, 1),
                rows(-2) + rows(2) + rows(0, -2) + rows(0, 2),
            )
            out[c, e] = 2.0 * here - middle[c, e] + speed_sq[e] * total
        return carry

    lax.fori_loop(0, 3, component, 0)


def corner_kernel(
    last, speed_sq, far_pair, near_pair, low_pair, high_pair, low_corner, high_corner, out
):
    west, east = east_layers(low_pair, high_pair)
    south, north = north_rows(near_pair, far_pair)
    odd = (lax.axis_index("east") & 1) == 1
    low, high = low_corner[...], high_corner[...]
    weight = {1: NEAR, 2: FAR}
    out[...] = last[...]
    for column, corner, e0, e_step in (
        (west, jnp.where(odd, low, high), 0, 1), (east, jnp.where(odd, high, low), CE - 1, -1)
    ):
        for rows, n0, n_step, first in ((south, 0, 1, 0), (north, CN - 1, -1, 2)):
            for e_in in range(2):
                e = e0 + e_in * e_step
                beside = rows(N_SPEED + e * 2, 2)
                for n_in in range(2):
                    n = n0 + n_in * n_step
                    for c in range(3):
                        total = jnp.zeros((1, CZ), jnp.float32)
                        for i in range(1, 3 - e_in):
                            k = 2 - i if e0 == 0 else i - 1
                            for j in range(1, 3 - n_in):
                                r = 2 - j if n0 == 0 else j - 1
                                at = (c * 2 + k) * 4 + first + r
                                speeds = column(E_SPEED + k, n) + beside[r : r + 1, :]
                                total += (weight[e_in + i] * weight[n_in + j]) * corner[at : at + 1, :] * speeds
                        out[c, e, n : n + 1, :] += speed_sq[e, n : n + 1, :] * total


def spread_kernel(parts, _, out):
    total = jnp.sum(parts[...], axis=0)
    for row in range(ROWS):
        out[row * PER_ROW : (row + 1) * PER_ROW] = jnp.broadcast_to(
            total[row : row + 1][None], (PER_ROW, 1, CZ)
        )


def own_kernel(parts, out):
    total = jnp.sum(parts[...], axis=0)
    at = lax.axis_index("east") & (PER_ROW - 1)
    turned = pltpu.roll(total, (CZ - at * PATCH_DEV) & (CZ - 1), 1)
    out[...] = turned[:, 0:PATCH_DEV]


def body(field_prev, field_now, speed_sq, mechanism, sub_cells, sub_patch):
    params = pltpu.CompilerParams(vmem_limit_bytes=LIMIT)
    f32 = jnp.float32
    field = pltpu.VMEM((3, CE, CN, CZ), f32)
    held = field, field, pltpu.VMEM((CE, CN, CZ), f32)
    east_message, north_message = pltpu.VMEM((E_LEN, 8, CZ), f32), pltpu.VMEM((N_LEN, CZ), f32)
    inputs = [
        pltpu.with_memory_space_constraint(x, pltpu.HBM)
        for x in (
            field_prev, field_now, speed_sq, mechanism, sub_cells,
            sub_cells.reshape(1, SUBS), sub_patch.reshape(1, SUBS), sub_patch,
        )
    ]
    i32 = jnp.int32
    ahead, field_now, speed_sq, far, near, low_pair, high_pair = pl.pallas_call(
        load_kernel, out_shape=[*held] + [north_message] * 2 + [east_message] * 2,
        in_specs=[HBM] * 7, out_specs=[VMEM] * 7,
        scratch_shapes=[
            field, pltpu.VMEM((CE, CN + 16, CZ), f32), pltpu.VMEM((6, SUBS), f32), pltpu.SMEM((SUBS,), i32),
            pltpu.VMEM((1, SUBS), i32), pltpu.VMEM((1, SUBS), i32), pltpu.SemaphoreType.DMA((11,)),
        ],
        compiler_params=params, name="load",
    )(*inputs[:7])
    far_pair = swap(far, "north", 1)
    near_pair = swap(near, "north", 0)
    halos = far_pair, near_pair, swap(low_pair, "east", 0), swap(high_pair, "east", 1)
    later = pltpu.VMEM((3, LAYERS, CN + 2 * TOP, CZ), f32)
    parts = pltpu.VMEM((COLUMN, ROWS, CZ), f32)
    corner = pltpu.VMEM((C_LEN, CZ), f32)
    field_next, later, parts = pl.pallas_call(
        steps_kernel,
        out_shape=[pltpu.HBM((3, CE, CN, CZ), f32), later, parts],
        in_specs=[VMEM] * 7 + [HBM] * 3, out_specs=[HBM] + [VMEM] * 2,
        scratch_shapes=[
            pltpu.VMEM((4, 3, 16, CZ), f32),
            pltpu.SMEM((6, SUBS), f32), pltpu.SMEM((SUBS,), i32), pltpu.SMEM((SUBS,), i32),
            pltpu.SMEM((4, S_LEN, CZ), f32), pltpu.VMEM((8, CZ), i32), pltpu.SMEM((8, CZ), i32),
            pltpu.SemaphoreType.DMA((8,)), pltpu.SemaphoreType.DMA((3,)),
        ],
        compiler_params=params, name="steps",
    )(ahead, field_now, speed_sq, *halos, inputs[3], inputs[4], inputs[7])
    low_corner, high_corner = pl.pallas_call(
        corner_strips_kernel, out_shape=[corner, corner], in_specs=[VMEM] * 3, out_specs=[VMEM] * 2,
        compiler_params=params, name="corner_strips",
    )(far_pair, near_pair, later)
    corners = swap(low_corner, "east", 0), swap(high_corner, "east", 1)
    field_last = pl.pallas_call(
        last_kernel, out_shape=pltpu.VMEM((3, CE, CN, CZ), f32), in_specs=[VMEM] * 3, out_specs=VMEM,
        compiler_params=params, name="last",
        cost_estimate=pl.CostEstimate(flops=3_000_000, bytes_accessed=1_000_000, transcendentals=0),
    )(field_now, speed_sq, later)
    parts = lax.all_to_all(parts, BOTH, 0, 0, tiled=True, axis_index_groups=column_groups())
    parts = pl.pallas_call(
        spread_kernel, out_shape=pltpu.VMEM((PLANE, 1, CZ), f32),
        in_specs=[VMEM] * 2, out_specs=VMEM, compiler_params=params, name="spread",
    )(parts, corners[1])
    parts = lax.all_to_all(parts, BOTH, 0, 0, tiled=True, axis_index_groups=plane_groups())
    own = pl.pallas_call(
        own_kernel, out_shape=jax.ShapeDtypeStruct((1, PATCH_DEV), f32),
        in_specs=[VMEM], out_specs=VMEM, compiler_params=params, name="own",
    )(parts)
    field_last = pl.pallas_call(
        corner_kernel, out_shape=jax.ShapeDtypeStruct((3, CE, CN, CZ), f32), in_specs=[VMEM] * 8,
        out_specs=VMEM, compiler_params=params, name="corners",
    )(field_last, speed_sq, *halos, *corners)
    return field_next, field_last, own.reshape(PATCH_DEV)


def solution(mesh):
    in_specs = (
        P(None, "east", "north", None),
        P(None, "east", "north", None),
        P("east", "north", None),
        P(None, BOTH),
        P(BOTH),
        P(BOTH),
    )
    out_specs = (
        P(None, "east", "north", None),
        P(None, "east", "north", None),
        P(BOTH),
    )
    return jax.shard_map(body, mesh=mesh, in_specs=in_specs, out_specs=out_specs, check_vma=False)
```
